128 devices in a mesh: section: 16 (over x, y_hi, core), expert: 8 (over z, y_lo).
Axes of the slice: x: 4, y: 4 (y_hi: 2, y_lo: 2; y = y_hi * 2 + y_lo), z: 4, core: 2. Of those that a mesh axis runs over, the one named last changes fastest.
Arguments:
- resid: bfloat16 [768, 6144], P('expert', 'section'), may hold values from -6 to 6
- query: bfloat16 [768, 6144], P('section', 'expert'), may hold values from -300 to 300, as said below
- new_keys: bfloat16 [768, 1024], P('section', 'expert'), may hold values from -6 to 6
- new_values: bfloat16 [768, 1024], P('section', 'expert'), may hold values from -6 to 6
- cache_keys: bfloat16 [128, 1024, 1024], P('section', None, 'expert'), may hold values from -6 to 6
- cache_values: bfloat16 [128, 1024, 1024], P('section', None, 'expert'), may hold values from -6 to 6
- cache_len: int32 [128], P('section'), may hold values from 1 to 1024, as said below
- out_weight: bfloat16 [6144, 6144], P('expert', 'section'), may hold values from -0.078125 to 0.078125
- expert_ids: int32 [768, 2], replicated, may hold values from 0 to 7, all different within a row; in each aligned block of 96 rows (0 to 95, 96 to 191, ...) at most 30 rows name the same one
- gates: float32 [768, 2], P('expert'), may hold values from 0.05 to 0.95, as said below
- w_gate: bfloat16 [8, 6144, 8192], P('expert', None, 'section'), may hold values from -0.078125 to 0.078125
- w_up: bfloat16 [8, 6144, 8192], P('expert', None, 'section'), may hold values from -0.078125 to 0.078125
- w_down: bfloat16 [8, 8192, 6144], P('expert', 'section'), may hold values from -0.0625 to 0.0625
Outputs:
- layer_out: bfloat16 [768, 6144], P('expert', 'section')
The draws below stay inside these ranges and needn't reach their ends.
Inputs may be any that keep to these rules, and one draw needn't show every extreme that they name: `query`: some queries may be far larger than typical. `cache_len`: at least one request's cache holds all 1024 positions. `expert_ids`: each row names two different experts; in each aligned block of 96 rows no expert is named by more than 30 rows. `gates`: the two gate weights of a row are positive and sum to one.
All inputs are finite; a program needn't handle non-finite values.
Results may differ from the reference program's by a relative error of at most 0.0055.
Values may be sent and summed in bfloat16 or wider, within the bound.
A program may use at most 128 MiB of HBM per device.

```python
import math
import jax
import jax.numpy as jnp
import numpy as np
from jax import lax

D = 6144
FF = 8192
HQ = 48
KV = 8
HD = 128
TOP = 2
DRAFT = 6
CACHE = 1024
EXPERTS = 8
REQ = 128
ROWS = 768
ROWS_BLK = 96
CAP = 30


def draw_query(key, part):
    key = jax.random.fold_in(key, 1)
    values = jnp.clip(jax.random.normal(key, (ROWS, HQ * HD), jnp.float32), -6.0, 6.0)
    return values.astype(jnp.bfloat16)


def draw_cache_len(key, part):
    key = jax.random.fold_in(key, 5)
    lengths = jax.random.randint(key, (REQ,), 1, CACHE + 1)
    longest = jax.random.randint(jax.random.fold_in(key, 6), (), 0, REQ)
    return lengths.at[longest].set(CACHE).astype(jnp.int32)


def draw_gates(key, part):
    key = jax.random.fold_in(key, 7)
    leading = jax.random.uniform(key, (ROWS,), jnp.float32, minval=0.5, maxval=0.95)
    return jnp.stack([leading, 1.0 - leading], axis=1).astype(jnp.float32)


def level_of(stream_key, extent, pieces, least, high):
    def one(axis_at, parts):
        steps = jax.random.uniform(jax.random.fold_in(jax.random.fold_in(stream_key, 6), axis_at), (parts,), jnp.float32, least / len(pieces), high / len(pieces))
        return jnp.repeat(jnp.exp(steps), extent[axis_at] // parts).reshape((-1,) + (1,) * (len(extent) - axis_at - 1))

    factor_of = one(*pieces[0])
    for cut in pieces[1:]:
        factor_of = factor_of * one(*cut)
    return factor_of


def shared_out(stream_key, own, number, rows, count, top, reach, skew):
    order = jax.random.permutation(stream_key, count)
    packed, ordinary = load_shares(count, rows * top, reach, skew, True), load_shares(count, rows * top, reach, skew, False)
    places = jnp.arange(count)

    def named(sizes, turn):
        used = int((sizes > 0).sum())
        fixed = max(1, used // 4)
        passed = fixed + (places - fixed + turn * (used - fixed)) % max(1, count - fixed)
        return jnp.zeros((count,), jnp.int32).at[order[jnp.where(places < fixed, places, passed)]].set(jnp.asarray(sizes, jnp.int32))

    sizes = jnp.where(number % 4 == 0, named(packed, number // 4), named(ordinary, number - number // 4 - 1))
    mixed = jax.random.permutation(jax.random.fold_in(own, 3), count)
    giver, sink = mixed[0:count // 2 * 2:2], mixed[1:count // 2 * 2:2]
    room = jnp.minimum(sizes[giver] - 1, reach - sizes[sink]) // 2
    room = jnp.where((giver == order[0]) | (sink == order[0]) | (sizes[sink] == 0), 0, jnp.maximum(room, 0))
    passed = jax.random.randint(jax.random.fold_in(own, 4), (count // 2,), 0, 1 << 20) % (room + 1)
    sizes = sizes.at[giver].add(-passed).at[sink].add(passed)
    items = jnp.searchsorted(jnp.cumsum(sizes), jnp.arange(rows * top), side="right").astype(jnp.int32)
    grid = items.reshape(top, rows).T
    grid = grid[jax.random.permutation(jax.random.fold_in(own, 1), rows)]
    turn = jax.random.randint(jax.random.fold_in(own, 2), (rows, 1), 0, top)
    return jnp.take_along_axis(grid, (jnp.arange(top)[None, :] + turn) % top, axis=1)


def load_shares(number_of, total, bound, slope, full):
    portions = [(1 << 20) // math.isqrt(rank ** slope) + 1 for rank in range(1, number_of + 1)]
    largest = bound if full else min(bound, max(-(-total // number_of), total * portions[0] // sum(portions)))
    least = 1 if total - largest >= number_of - 1 else 0
    counts, surplus = [largest] + [least] * (number_of - 1), total - largest - least * (number_of - 1)
    while surplus > 0:
        free = [i for i in range(1, number_of) if counts[i] < largest] or [i for i in range(1, number_of) if counts[i] < bound]
        mass, left = sum([portions[i] for i in free]), surplus
        for i in free:
            more = min(bound - counts[i], max(1, left * portions[i] // mass), surplus)
            counts[i] = counts[i] + more
            surplus = surplus - more
    return np.array(counts)


def scatter_about(rng, extent, spread, reach, split=(), held_as=jnp.bfloat16):
    array = spread * jax.random.normal(rng, extent, jnp.float32)
    if split:
        array = array * level_of(rng, extent, split, -0.22, 0.18)
    return jnp.clip(array, -reach, reach).astype(held_as)


def setup_inputs(seed: int = 0) -> dict:
    key_of = jax.random.split(jax.random.key(seed), 14)
    resid = scatter_about(key_of[0], (ROWS, D), 1.0, 6.0, ((0, 8), (1, 16)))
    query = draw_query(jax.random.fold_in(key_of[13], 71), 0)
    new_keys = scatter_about(key_of[2], (ROWS, KV * HD), 1.0, 6.0, ((0, 16), (1, 8)))
    new_values = scatter_about(key_of[3], (ROWS, KV * HD), 1.0, 6.0, ((0, 16), (1, 8)))
    cache_keys = scatter_about(key_of[4], (REQ, CACHE, KV * HD), 1.0, 6.0, ((0, 16), (2, 8)))
    cache_values = scatter_about(key_of[5], (REQ, CACHE, KV * HD), 1.0, 6.0, ((0, 16), (2, 8)))
    cache_len = draw_cache_len(jax.random.fold_in(key_of[13], 71), 0)
    out_weight = scatter_about(key_of[7], (HQ * HD, D), (HQ * HD) ** -0.5, 0.078125, ((0, 8), (1, 16)))
    expert_ids_keys = jax.random.split(jax.random.fold_in(key_of[8], 1), ROWS // ROWS_BLK)
    expert_ids_turns = jax.random.permutation(jax.random.fold_in(key_of[8], 3), ROWS // ROWS_BLK)
    expert_ids = jax.vmap(lambda own, number: shared_out(jax.random.fold_in(key_of[8], 2), own, number, ROWS_BLK, EXPERTS, TOP, CAP, 2))(expert_ids_keys, expert_ids_turns).reshape((ROWS, TOP))
    gates = draw_gates(jax.random.fold_in(key_of[13], 71), 0)
    w_gate = scatter_about(key_of[10], (EXPERTS, D, FF), D ** -0.5, 0.078125, ((0, 8), (2, 16)))
    w_up = scatter_about(key_of[11], (EXPERTS, D, FF), D ** -0.5, 0.078125, ((0, 8), (2, 16)))
    w_down = scatter_about(key_of[12], (EXPERTS, FF, D), FF ** -0.5, 0.0625, ((0, 8), (1, 16)))
    return dict(resid=resid, query=query, new_keys=new_keys, new_values=new_values, cache_keys=cache_keys, cache_values=cache_values, cache_len=cache_len, out_weight=out_weight, expert_ids=expert_ids, gates=gates, w_gate=w_gate, w_up=w_up, w_down=w_down)


def attend_request(operands):
    queries, draft_keys, draft_values, past_keys, past_values, length = operands
    groups = HQ // KV
    scale = 1.0 / math.sqrt(HD)
    qmat = queries.astype(jnp.float32).reshape(DRAFT, KV, groups, HD)
    past_k = past_keys.astype(jnp.float32).reshape(CACHE, KV, HD)
    past_v = past_values.astype(jnp.float32).reshape(CACHE, KV, HD)
    new_k = draft_keys.astype(jnp.float32).reshape(DRAFT, KV, HD)
    new_v = draft_values.astype(jnp.float32).reshape(DRAFT, KV, HD)
    past_scores = jnp.einsum('dkgh,ckh->kgdc', qmat, past_k) * scale
    valid = jnp.arange(CACHE, dtype=jnp.int32) < length
    past_scores = jnp.where(valid[None, None, None, :], past_scores, -1e+30)
    new_scores = jnp.einsum('dkgh,ekh->kgde', qmat, new_k) * scale
    causal = jnp.arange(DRAFT)[:, None] >= jnp.arange(DRAFT)[None, :]
    new_scores = jnp.where(causal[None, None], new_scores, -1e+30)
    top_score = jnp.maximum(lax.optimization_barrier(jnp.max(past_scores, axis=-1)), lax.optimization_barrier(jnp.max(new_scores, axis=-1)))
    past_exp = jnp.exp(past_scores - top_score[..., None])
    new_exp = jnp.exp(new_scores - top_score[..., None])
    total = lax.optimization_barrier(jnp.sum(past_exp, axis=-1)) + lax.optimization_barrier(jnp.sum(new_exp, axis=-1))
    past_prob = (past_exp / total[..., None]).astype(jnp.bfloat16).astype(jnp.float32)
    new_prob = (new_exp / total[..., None]).astype(jnp.bfloat16).astype(jnp.float32)
    mixed = jnp.einsum('kgdc,ckh->dkgh', past_prob, past_v) + jnp.einsum('kgde,ekh->dkgh', new_prob, new_v)
    return mixed.reshape(DRAFT, HQ * HD).astype(jnp.bfloat16)

def run_expert(operands):
    buffer, gate_w, up_w, down_w = operands
    gate_acc = jnp.dot(buffer, gate_w, preferred_element_type=jnp.float32)
    up_acc = jnp.dot(buffer, up_w, preferred_element_type=jnp.float32)
    activated = (jax.nn.silu(gate_acc) * up_acc).astype(jnp.bfloat16)
    return jnp.dot(activated, down_w, preferred_element_type=jnp.float32)

def reference(resid, query, new_keys, new_values, cache_keys, cache_values, cache_len, out_weight, expert_ids, gates, w_gate, w_up, w_down):
    attended = lax.map(attend_request, (query.reshape(REQ, DRAFT, HQ * HD), new_keys.reshape(REQ, DRAFT, KV * HD), new_values.reshape(REQ, DRAFT, KV * HD), cache_keys, cache_values, cache_len))
    attended = attended.reshape(ROWS, HQ * HD)
    projected = jnp.dot(attended, out_weight, preferred_element_type=jnp.float32)
    hidden_in = (resid.astype(jnp.float32) + projected).astype(jnp.bfloat16)
    blocks = EXPERTS
    flat = expert_ids.reshape(blocks, ROWS_BLK * TOP)
    onehot = (flat[..., None] == jnp.arange(EXPERTS, dtype=jnp.int32)).astype(jnp.int32)
    slot = lax.optimization_barrier(jnp.sum((jnp.cumsum(onehot, axis=1) - onehot) * onehot, axis=-1))
    block_idx = jnp.arange(blocks, dtype=jnp.int32)[:, None]
    position = (flat * (blocks * CAP) + block_idx * CAP + slot).reshape(ROWS, TOP).astype(jnp.int32)
    row_idx = jnp.broadcast_to(jnp.arange(ROWS, dtype=jnp.int32)[:, None], (ROWS, TOP))
    buffer_rows = jnp.full((EXPERTS * blocks * CAP,), ROWS, jnp.int32).at[position.reshape(-1)].set(row_idx.reshape(-1))
    padded = jnp.concatenate([hidden_in, jnp.zeros((1, D), jnp.bfloat16)], axis=0)
    buffers = padded[buffer_rows].reshape(EXPERTS, blocks * CAP, D)
    outputs = lax.map(run_expert, (buffers, w_gate, w_up, w_down)).reshape(EXPERTS * blocks * CAP, D)
    picked = outputs[position]
    mixture = lax.optimization_barrier(jnp.sum(gates[..., None] * picked, axis=1))
    return (hidden_in.astype(jnp.float32) + mixture).astype(jnp.bfloat16)
```

```python
import functools
import math

import jax
import jax.numpy as jnp
import numpy as np
from jax import lax
from jax.experimental import pallas as pl
from jax.experimental.pallas import tpu as pltpu
from jax.sharding import PartitionSpec as P

MESH = pl.DeviceIdType.MESH
BF = jnp.bfloat16
F32 = jnp.float32

GROUPS = 6
HD = 128
DRAFT = 6
REQS = 8
SROWS = 48
PADQ = 48
CACHE = 1024
BLK = 96
CAPP = 32
EXP = 8
CHIPS = 8
SEC = 16
BUF = EXP * CAPP
FEAT = 384
D = 6144
HID = 512
NEG = -1e30


def constants():
    pick = np.zeros((REQS * PADQ, GROUPS * SROWS), np.float32)
    mask = np.zeros((REQS * PADQ, SROWS), np.float32)
    for r in range(REQS):
        for g in range(GROUPS):
            for d in range(DRAFT):
                i = r * PADQ + g * DRAFT + d
                pick[i, g * SROWS + r * DRAFT + d] = 1.0
                mask[i, r * DRAFT : r * DRAFT + d + 1] = 1.0
    return pick, mask


def dot(a, b):
    return jnp.dot(a, b, preferred_element_type=F32)


def dot_t(a, b):
    return lax.dot_general(a, b, (((1,), (1,)), ((), ())), preferred_element_type=F32)


def kernel(
    clen,
    resid_h, query_h, nk_h, nv_h, ck_h, cv_h, ow_h, ids_h, gates_h, wg_h, wu_h, wd_h, pick_h, unpick_h, mask_h,
    out_ref,
    resid, query, nk, nv, ck, cv, ow, ids, gates, wg, wu, wd, pick, unpick, mask,
    qp, snew, att, proj_s, proj_r, hidden, comb, disp_s, big, acc, act,
    pair_s, pair_r, mine, red_s, mid_r, fin_r, ret_s, ret,
    lsem, att_ss, att_rs, proj_ss, proj_rs, disp_ss, disp_rs, big_ss, big_rs,
    pair_ss, pair_rs, red_ss, mid_rs, fin_rs, ret_ss, ret_rs,
):
    s = lax.axis_index("section")
    e = lax.axis_index("expert")
    core = lax.rem(s, 2)
    chip = s // 2
    x, yh = chip // 2, lax.rem(chip, 2)

    def at(dx, dy):
        return lax.rem(x + dx + 4, 4) * 2 + lax.rem(yh + dy, 2)

    def lane(q):
        return (q * 2 + core, e)

    other = (chip * 2 + 1 - core, e)

    loads = [(query_h, query), (pick_h, pick), (nk_h, nk), (mask_h, mask)]
    loads += [(ck_h.at[r], ck.at[r]) for r in range(REQS)]
    loads += [(nv_h, nv)]
    loads += [(cv_h.at[r], cv.at[r]) for r in range(REQS)]
    loads += [(unpick_h, unpick), (ow_h, ow), (ids_h.at[pl.ds(pl.multiple_of(e * BLK, BLK), BLK)], ids)]
    loads += [(gates_h, gates), (resid_h, resid)]
    loads += [(wg_h.at[0], wg), (wu_h.at[0], wu)]
    loads += [(wd_h.at[0, :, pl.ds(q * 2 * FEAT, 2 * FEAT)], wd.at[q]) for q in range(CHIPS)]
    local = [pltpu.make_async_copy(a, b, lsem.at[i]) for i, (a, b) in enumerate(loads)]
    for cp in local:
        cp.start()
    (l_query, l_pick, l_nk, l_mask), l_ck = local[:4], local[4:12]
    l_nv, l_cv = local[12], local[13:21]
    l_unpick, l_ow, l_ids, l_gates, l_resid, l_wg, l_wu = local[21:28]
    l_wd = local[28:36]

    bar = pltpu.get_barrier_semaphore()
    ring = [(1, 0), (3, 0), (2, 0), (0, 1)]
    partners = [lane(at(dx, dy)) for dx, dy in ring] + [other]
    partners += [(s, lax.rem(e + k, EXP)) for k in range(1, EXP)]
    for p in partners:
        pl.semaphore_signal(bar, 1, device_id=p, device_id_type=MESH)

    l_query.wait()
    l_pick.wait()
    stacked = jnp.concatenate([query[:, g * HD : (g + 1) * HD] for g in range(GROUPS)], axis=0)
    qp[...] = dot(pick[...], stacked).astype(BF)
    l_nk.wait()
    l_mask.wait()
    scale = 1.0 / math.sqrt(HD)
    snew[...] = jnp.where(mask[...] > 0.5, dot_t(qp[...], nk[...]) * scale, NEG)
    col = lax.broadcasted_iota(jnp.int32, (PADQ, CACHE), 1)
    l_nv.wait()
    l_unpick.wait()
    mixed = []
    for r in range(REQS):
        l_ck[r].wait()
        rows = pl.ds(r * PADQ, PADQ)
        sc = dot_t(qp[rows, :], ck[r]) * scale
        sc = jnp.where(col < clen[r], sc, NEG)
        sn = snew[rows, :]
        top = jnp.maximum(jnp.max(sc, axis=1, keepdims=True), jnp.max(sn, axis=1, keepdims=True))
        pe = jnp.exp(sc - top)
        ne = jnp.exp(sn - top)
        inv = 1.0 / (jnp.sum(pe, axis=1, keepdims=True) + jnp.sum(ne, axis=1, keepdims=True))
        l_cv[r].wait()
        mixed.append((dot((pe * inv).astype(BF), cv[r]) + dot((ne * inv).astype(BF), nv[...])).astype(BF))
    spread = dot(unpick[...], jnp.concatenate(mixed, axis=0)).astype(BF)
    for g in range(GROUPS):
        att[s, :, g * HD : (g + 1) * HD] = spread[g * SROWS : (g + 1) * SROWS]

    pl.semaphore_wait(bar, len(partners))

    def gather(buf, ss, rs):
        sends = []

        def send(q, dest):
            slot = q * 2 + core
            cp = pltpu.make_async_remote_copy(
                buf.at[slot], buf.at[slot], ss.at[len(sends)], rs.at[slot], device_id=dest, device_id_type=MESH
            )
            cp.start()
            sends.append(cp)

        def arrive(slot):
            pltpu.make_async_remote_copy(
                buf.at[slot], buf.at[slot], ss.at[0], rs.at[slot], device_id=other, device_id_type=MESH
            ).wait_recv()

        def first():
            for d in ((0, 1), (2, 0), (1, 0), (3, 0)):
                send(chip, lane(at(*d)))
            send(chip, other)
            arrive(chip * 2 + 1 - core)

        def mine_in(dx, dy):
            q = at(dx, dy)
            arrive(q * 2 + core)
            if (dx, dy) == (0, 1):
                send(q, lane(at(1, 0)))
                send(q, lane(at(3, 0)))
            if (dx, dy) == (2, 0):
                send(q, lane(at(0, 1)))
            send(q, other)

        def theirs_in(dx, dy):
            arrive(at(dx, dy) * 2 + 1 - core)

        return first, mine_in, theirs_in, sends

    def run_gather(buf, ss, rs, use):
        first, mine_in, theirs_in, sends = gather(buf, ss, rs)
        first()
        use(chip)
        level = ((0, 1), (1, 0), (3, 0), (2, 0))
        for d in level:
            mine_in(*d)
        for d in level:
            theirs_in(*d)
            use(at(*d))
        level = ((1, 1), (3, 1), (2, 1))
        for d in level:
            mine_in(*d)
        for d in level:
            theirs_in(*d)
            use(at(*d))
        return sends

    l_ow.wait()
    pending = []

    def project(q):
        rows = jnp.concatenate([att[q * 2], att[q * 2 + 1]], axis=0)
        proj_s[q] = dot(rows, ow[...]).astype(BF)

        @pl.when(q != e)
        def _():
            pltpu.make_async_remote_copy(
                proj_s.at[q], proj_r.at[e], proj_ss.at[q], proj_rs.at[e], device_id=(s, q), device_id_type=MESH
            ).start()

    pending += run_gather(att, att_ss, att_rs, project)

    l_ids.wait()
    l_gates.wait()
    jv = lax.broadcasted_iota(jnp.int32, (BLK, BUF), 1)
    expert_of = jv // CAPP
    slot_of = lax.rem(jv, CAPP)
    n0 = ids[:, 0:1] == expert_of
    n1 = ids[:, 1:2] == expert_of
    named = jnp.where(n0 | n1, 1.0, 0.0)
    lower = jnp.where(
        lax.broadcasted_iota(jnp.int32, (BLK, BLK), 0) > lax.broadcasted_iota(jnp.int32, (BLK, BLK), 1), 1.0, 0.0
    ).astype(BF)
    earlier = dot(lower, named.astype(BF))
    place = jnp.where(earlier == slot_of.astype(F32), named, 0.0)
    comb[...] = place * (jnp.where(n0, gates[:, 0:1], 0.0) + jnp.where(n1, gates[:, 1:2], 0.0))
    picker = jnp.transpose(place).astype(BF)

    l_resid.wait()
    total = resid[...].astype(F32) + proj_s[e].astype(F32)
    for k in range(1, EXP):
        src = lax.rem(e + k, EXP)
        pltpu.make_async_remote_copy(
            proj_s.at[src], proj_r.at[src], proj_ss.at[src], proj_rs.at[src], device_id=(s, src), device_id_type=MESH
        ).wait_recv()
        total = total + proj_r[src].astype(F32)
    hid = total.astype(BF)
    hidden[...] = hid

    disp_s[...] = dot(picker, hid).astype(BF).reshape(EXP, CAPP, FEAT)
    my_rows = pl.ds(pl.multiple_of(e * CAPP, CAPP), CAPP)
    for k in range(1, EXP):
        d = lax.rem(e + k, EXP)
        cp = pltpu.make_async_remote_copy(
            disp_s.at[d], big.at[s, my_rows], disp_ss.at[k], disp_rs.at[e], device_id=(s, d), device_id_type=MESH
        )
        cp.start()
        pending.append(cp)
    big[s, my_rows, :] = disp_s[e]
    for k in range(1, EXP):
        src = lax.rem(e + k, EXP)
        rows = pl.ds(pl.multiple_of(src * CAPP, CAPP), CAPP)
        pltpu.make_async_remote_copy(
            disp_s.at[src], big.at[s, rows], disp_ss.at[k], disp_rs.at[src], device_id=(s, src), device_id_type=MESH
        ).wait_recv()

    l_wg.wait()
    l_wu.wait()
    done = []

    def up(q):
        rows = jnp.concatenate([big[q * 2], big[q * 2 + 1]], axis=1)
        feats = pl.ds(pl.multiple_of(q * 2 * FEAT, 2 * FEAT), 2 * FEAT)
        ga, ua = dot(rows, wg[feats, :]), dot(rows, wu[feats, :])
        if done:
            acc[0] += ga
            acc[1] += ua
        else:
            acc[0] = ga
            acc[1] = ua
        done.append(q)

    pending += run_gather(big, big_ss, big_rs, up)
    g = acc[0]
    act[...] = (g / (1.0 + jnp.exp(-g)) * acc[1]).astype(BF)

    for cp in l_wd:
        cp.wait()
    order = [(1, 1), (3, 1), (2, 1), (1, 0), (3, 0), (2, 0), (0, 1), (0, 0)]

    def down(i):
        p = dot(act[...], wd[at(*order[i])])
        lo, hi = p[:, :FEAT], p[:, FEAT:]
        mine[i] = jnp.where(core == 0, lo, hi)
        pair_s[i] = jnp.where(core == 0, hi, lo).astype(BF)
        cp = pltpu.make_async_remote_copy(
            pair_s.at[i], pair_r.at[i], pair_ss.at[i], pair_rs.at[i], device_id=other, device_id_type=MESH
        )
        cp.start()
        pending.append(cp)

    def paired(i):
        pltpu.make_async_remote_copy(
            pair_s.at[i], pair_r.at[i], pair_ss.at[i], pair_rs.at[i], device_id=other, device_id_type=MESH
        ).wait_recv()
        return mine[i] + pair_r[i].astype(F32)

    def landed(buf, rs, j):
        pltpu.make_async_remote_copy(
            red_s.at[0], buf.at[j], red_ss.at[0], rs.at[j], device_id=other, device_id_type=MESH
        ).wait_recv()
        return buf[j].astype(F32)

    def push(i, value, dest, buf, rs, j):
        red_s[i] = value.astype(BF)
        cp = pltpu.make_async_remote_copy(
            red_s.at[i], buf.at[j], red_ss.at[i], rs.at[j], device_id=lane(at(*dest)), device_id_type=MESH
        )
        cp.start()
        pending.append(cp)

    def finish(i):
        v = paired(i)
        if i == 0:
            push(0, v, (1, 0), mid_r, mid_rs, 0)
        elif i == 1:
            push(1, v, (3, 0), mid_r, mid_rs, 1)
        elif i == 2:
            push(2, v, (0, 1), mid_r, mid_rs, 2)
        elif i == 3:
            push(3, v, (1, 0), fin_r, fin_rs, 0)
        elif i == 4:
            push(4, v, (3, 0), fin_r, fin_rs, 1)
        elif i == 5:
            push(5, v + landed(mid_r, mid_rs, 2), (2, 0), fin_r, fin_rs, 2)
        elif i == 6:
            push(6, v + landed(mid_r, mid_rs, 0) + landed(mid_r, mid_rs, 1), (0, 1), fin_r, fin_rs, 3)
        else:
            for j in range(4):
                v = v + landed(fin_r, fin_rs, j)
        return v

    down(0)
    for i in range(1, CHIPS):
        down(i)
        finish(i - 1)
    ret_s[...] = finish(CHIPS - 1).astype(BF)

    for k in range(1, EXP):
        d = lax.rem(e + k, EXP)
        rows = pl.ds(pl.multiple_of(d * CAPP, CAPP), CAPP)
        cp = pltpu.make_async_remote_copy(
            ret_s.at[rows], ret.at[my_rows], ret_ss.at[k], ret_rs.at[e], device_id=(s, d), device_id_type=MESH
        )
        cp.start()
        pending.append(cp)
    ret[my_rows, :] = ret_s[my_rows, :]
    w = comb[...]
    w_hi = w.astype(BF)
    w_lo = (w - w_hi.astype(F32)).astype(BF)
    for k in range(1, EXP):
        src = lax.rem(e + k, EXP)
        rows = pl.ds(pl.multiple_of(src * CAPP, CAPP), CAPP)
        pltpu.make_async_remote_copy(
            ret_s.at[rows], ret.at[rows], ret_ss.at[k], ret_rs.at[src], device_id=(s, src), device_id_type=MESH
        ).wait_recv()
    back = ret[...]
    out_ref[...] = (hidden[...].astype(F32) + (dot(w_hi, back) + dot(w_lo, back))).astype(BF)

    for cp in pending:
        cp.wait_send()
    for k in range(1, EXP):
        d = lax.rem(e + k, EXP)
        pltpu.make_async_remote_copy(
            proj_s.at[d], proj_r.at[d], proj_ss.at[d], proj_rs.at[d], device_id=(s, d), device_id_type=MESH
        ).wait_send()


def per_device(
    resid, query, new_keys, new_values, cache_keys, cache_values, cache_len, out_weight,
    expert_ids, gates, w_gate, w_up, w_down,
):
    pick, mask = constants()
    V = pltpu.VMEM
    S = pltpu.SemaphoreType.DMA
    scratch = [
        V((BLK, FEAT), BF), V((SROWS, 768), BF), V((SROWS, HD), BF), V((SROWS, HD), BF),
        V((REQS, CACHE, HD), BF), V((REQS, CACHE, HD), BF), V((768, FEAT), BF),
        V((BLK, 2), jnp.int32), V((BLK, 2), F32),
        V((D, HID), BF), V((D, HID), BF), V((CHIPS, HID, 2 * FEAT), BF),
        V(pick.shape, BF), V(pick.T.shape, BF), V(mask.shape, F32),
        V((REQS * PADQ, HD), BF), V((REQS * PADQ, SROWS), F32),
        V((SEC, SROWS, 768), BF),
        V((EXP, BLK, FEAT), BF), V((EXP, BLK, FEAT), BF),
        V((BLK, FEAT), BF), V((BLK, BUF), F32),
        V((EXP, CAPP, FEAT), BF), V((SEC, BUF, FEAT), BF),
        V((2, BUF, HID), F32), V((BUF, HID), BF),
        V((CHIPS, BUF, FEAT), BF), V((CHIPS, BUF, FEAT), BF), V((CHIPS, BUF, FEAT), F32),
        V((CHIPS, BUF, FEAT), BF), V((3, BUF, FEAT), BF), V((4, BUF, FEAT), BF),
        V((BUF, FEAT), BF), V((BUF, FEAT), BF),
        S((36,)), S((16,)), S((SEC,)), S((EXP,)), S((EXP,)), S((EXP,)), S((EXP,)), S((16,)), S((SEC,)),
        S((CHIPS,)), S((CHIPS,)), S((CHIPS,)), S((3,)), S((4,)), S((EXP,)), S((EXP,)),
    ]
    anyspec = pl.BlockSpec(memory_space=pl.ANY)
    return pl.pallas_call(
        kernel,
        out_shape=jax.ShapeDtypeStruct((BLK, FEAT), BF),
        in_specs=[pl.BlockSpec(memory_space=pltpu.SMEM)] + [anyspec] * 15,
        out_specs=pl.BlockSpec(memory_space=pltpu.VMEM),
        scratch_shapes=scratch,
        compiler_params=pltpu.CompilerParams(collective_id=0, has_side_effects=True, vmem_limit_bytes=60 << 20),
    )(
        cache_len, resid, query, new_keys, new_values, cache_keys, cache_values, out_weight, expert_ids, gates,
        w_gate, w_up, w_down, jnp.asarray(pick, BF), jnp.asarray(pick.T, BF), jnp.asarray(mask, F32),
    )


def solution(mesh):
    in_specs = (
        P("expert", "section"),
        P("section", "expert"),
        P("section", "expert"),
        P("section", "expert"),
        P("section", None, "expert"),
        P("section", None, "expert"),
        P("section"),
        P("expert", "section"),
        P(),
        P("expert", None),
        P("expert", None, "section"),
        P("expert", None, "section"),
        P("expert", "section", None),
    )
    return jax.shard_map(
        per_device, mesh=mesh, in_specs=in_specs, out_specs=P("expert", "section"), check_vma=False
    )
```

```python
import functools
import math

import jax
import jax.numpy as jnp
import numpy as np
from jax import lax
from jax.experimental import pallas as pl
from jax.experimental.pallas import tpu as pltpu
from jax.sharding import PartitionSpec as P

MESH = pl.DeviceIdType.MESH
BF = jnp.bfloat16
F32 = jnp.float32

GROUPS = 6
HD = 128
DRAFT = 6
REQS = 8
SROWS = 48
PADQ = 48
CACHE = 1024
BLK = 96
CAPP = 32
EXP = 8
CHIPS = 8
SEC = 16
BUF = EXP * CAPP
FEAT = 384
D = 6144
HID = 512
HALF = BUF // 2
NEG = -1e30
PART, FIRST, HOLD = (32, 16), (0, 32), ((0, 6), (5, 8))
NEAR = [(0, 0), (0, 1), (1, 0), (3, 0), (1, 1), (3, 1), (2, 0), (2, 1)]
ORDER = [(2, 1), (1, 1), (3, 1), (2, 0), (1, 0), (3, 0), (0, 1), (0, 0)]


def constants():
    pick = np.zeros((REQS * PADQ, GROUPS * SROWS), np.float32)
    mask = np.zeros((REQS * PADQ, SROWS), np.float32)
    for r in range(REQS):
        for g in range(GROUPS):
            for d in range(DRAFT):
                i = r * PADQ + g * DRAFT + d
                pick[i, g * SROWS + r * DRAFT + d] = 1.0
                mask[i, r * DRAFT : r * DRAFT + d + 1] = 1.0
    back = []
    for rows, first, (low, high) in zip(PART, FIRST, HOLD):
        cut = pick[low * PADQ : high * PADQ].reshape(-1, GROUPS, SROWS)[:, :, first : first + rows]
        back.append(cut.reshape(-1, GROUPS * rows).T)
    return pick, mask, *back


def dot(a, b):
    return jnp.dot(a, b, preferred_element_type=F32)


def dot_t(a, b):
    return lax.dot_general(a, b, (((1,), (1,)), ((), ())), preferred_element_type=F32)


def kernel(
    clen,
    resid_h, query_h, nk_h, nv_h, ck_h, cv_h, ow_h, ids_h, gates_h, wg_h, wu_h, wd_h, pick_h, back0_h, back1_h, mask_h,
    out_ref,
    resid, query, nk, nv, ck, cv, ow, ids, gates, wg, wu, wd, pick, back0, back1, mask,
    qp, snew, mixed, att0, att1, proj_s0, proj_s1, proj_r0, proj_r1, hidden, picker, comb, disp_s, big, acc, act,
    pair_s, pair_r, mine, red_s, mid_r, hop_r, fin_r, ret_s, ret,
    lsem, ow_ss, ow_rs, att_ss, att_rs, proj_ss, proj_rs, disp_ss, disp_rs, big_ss, big_rs, part_rs,
    pair_ss, pair_rs, red_ss, mid_rs, hop_rs, fin_rs, ret_ss, ret_rs,
):
    s = lax.axis_index("section")
    e = lax.axis_index("expert")
    core = lax.rem(s, 2)
    chip = s // 2
    x, yh = chip // 2, lax.rem(chip, 2)

    def at(dx, dy):
        return lax.rem(x + dx + 4, 4) * 2 + lax.rem(yh + dy, 2)

    def lane(q):
        return (q * 2 + core, e)

    other = (chip * 2 + 1 - core, e)

    loads = [(query_h, query), (pick_h, pick), (nk_h, nk), (mask_h, mask)]
    loads += [(ck_h.at[r], ck.at[r]) for r in range(REQS)]
    loads += [(nv_h, nv)]
    loads += [(cv_h.at[r], cv.at[r]) for r in range(REQS)]
    mine_ow = ow.at[:, pl.ds(pl.multiple_of(core * FEAT, HD), FEAT)]
    loads += [(back0_h, back0), (back1_h, back1), (ow_h, mine_ow), (ids_h, ids), (gates_h, gates), (resid_h, resid)]
    early = len(loads)
    loads += [(wg_h.at[0], wg), (wu_h.at[0], wu)]
    loads += [(wd_h.at[0, :, pl.ds(q * 2 * FEAT, 2 * FEAT)], wd.at[q]) for q in range(CHIPS)]
    local = [pltpu.make_async_copy(a, b, lsem.at[i]) for i, (a, b) in enumerate(loads)]
    for cp in local[:early]:
        cp.start()
    (l_query, l_pick, l_nk, l_mask), l_ck = local[:4], local[4:12]
    l_nv, l_cv = local[12], local[13:21]
    l_back, l_ow, l_ids, l_gates, l_resid, l_wg, l_wu = local[21:23], *local[23:29]
    l_wd = local[29:37]

    bar = pltpu.get_barrier_semaphore()
    ring = [(1, 0), (3, 0), (2, 0), (0, 1)]
    partners = [lane(at(dx, dy)) for dx, dy in ring] + [other]
    partners += [(d, lax.rem(e + k, EXP)) for k in range(1, EXP) for d in (s, other[0])]
    for p in partners:
        pl.semaphore_signal(bar, 1, device_id=p, device_id_type=MESH)

    l_query.wait()
    l_pick.wait()
    stacked = jnp.concatenate([query[:, g * HD : (g + 1) * HD] for g in range(GROUPS)], axis=0)
    qp[...] = dot(pick[...], stacked).astype(BF)
    l_nk.wait()
    l_mask.wait()
    scale = 1.0 / math.sqrt(HD)
    snew[...] = jnp.where(mask[...] > 0.5, dot_t(qp[...], nk[...]) * scale, NEG)
    col = lax.broadcasted_iota(jnp.int32, (PADQ, CACHE), 1)
    l_nv.wait()

    def attend(r):
        l_ck[r].wait()
        rows = pl.ds(r * PADQ, PADQ)
        sc = dot_t(qp[rows, :], ck[r]) * scale
        sc = jnp.where(col < clen[r], sc, NEG)
        sn = snew[rows, :]
        top = jnp.maximum(jnp.max(sc, axis=1, keepdims=True), jnp.max(sn, axis=1, keepdims=True))
        pe = jnp.exp(sc - top)
        ne = jnp.exp(sn - top)
        inv = 1.0 / (jnp.sum(pe, axis=1, keepdims=True) + jnp.sum(ne, axis=1, keepdims=True))
        l_cv[r].wait()
        mixed[rows, :] = (dot((pe * inv).astype(BF), cv[r]) + dot((ne * inv).astype(BF), nv[...])).astype(BF)

    att = (att0, att1)
    pending = []

    def arrive(dst, sem):
        pltpu.make_async_remote_copy(dst, dst, ow_ss, sem, device_id=other, device_id_type=MESH).wait_recv()

    def att_send(h, q, n, dest):
        piece = att[h].at[q]
        cp = pltpu.make_async_remote_copy(
            piece, piece, att_ss.at[h, n], att_rs.at[h, q], device_id=lane(at(*dest)), device_id_type=MESH
        )
        cp.start()
        pending.append(cp)

    def att_start(h):
        l_back[h].wait()
        low, high = HOLD[h]
        spread = dot((back0, back1)[h][...], mixed[low * PADQ : high * PADQ, :]).astype(BF)
        n = PART[h]
        for g in range(GROUPS):
            att[h][chip, :, g * HD : (g + 1) * HD] = spread[g * n : (g + 1) * n]
        for n, d in enumerate(((0, 1), (2, 0), (1, 0), (3, 0))):
            att_send(h, chip, n, d)

    def att_come(h, *d):
        q = at(*d)
        arrive(att[h].at[q], att_rs.at[h, q])
        if d == (0, 1):
            att_send(h, q, 4, (1, 0))
            att_send(h, q, 5, (3, 0))
        if d == (2, 0):
            att_send(h, q, 6, (0, 1))

    for r in range(HOLD[0][1]):
        attend(r)
    pl.semaphore_wait(bar, len(partners))
    l_ow.wait()
    cp = pltpu.make_async_remote_copy(mine_ow, mine_ow, ow_ss, ow_rs, device_id=other, device_id_type=MESH)
    cp.start()
    pending.append(cp)
    att_start(0)
    for r in range(HOLD[0][1], REQS):
        attend(r)
    att_start(1)

    for cp in local[early:]:
        cp.start()
    l_ids.wait()
    l_gates.wait()
    of_block = lax.broadcasted_iota(jnp.int32, (EXP * BLK, BLK), 0) == (
        lax.broadcasted_iota(jnp.int32, (EXP * BLK, BLK), 1) + e * BLK
    )
    named_by = dot(ids[...].astype(F32).astype(BF), jnp.where(of_block, 1.0, 0.0).astype(BF))
    jv = lax.broadcasted_iota(jnp.int32, (BUF, BLK), 0)
    expert_of = (jv // CAPP).astype(F32)
    slot_of = lax.rem(jv, CAPP).astype(F32)
    n0 = named_by[0:1, :] == expert_of
    n1 = named_by[1:2, :] == expert_of
    named = jnp.where(n0 | n1, 1.0, 0.0)
    upper = lax.broadcasted_iota(jnp.int32, (BLK, BLK), 0) < lax.broadcasted_iota(jnp.int32, (BLK, BLK), 1)
    earlier = dot(named.astype(BF), jnp.where(upper, 1.0, 0.0).astype(BF))
    place = jnp.where(earlier == slot_of, named, 0.0)
    picker[...] = place.astype(BF)
    weight = jnp.transpose(place * (jnp.where(n0, gates[0:1, :], 0.0) + jnp.where(n1, gates[1:2, :], 0.0)))
    comb[0] = weight.astype(BF)
    comb[1] = (weight - comb[0].astype(F32)).astype(BF)

    proj_s, proj_r = (proj_s0, proj_s1), (proj_r0, proj_r1)
    their_ow = ow.at[:, pl.ds(pl.multiple_of((1 - core) * FEAT, HD), FEAT)]
    arrive(their_ow, ow_rs)

    def proj_copy(h, q, c, frm):
        return pltpu.make_async_remote_copy(
            proj_s[h].at[q, c], proj_r[h].at[frm, core], proj_ss.at[h, q, c], proj_rs.at[h, frm, core],
            device_id=(chip * 2 + c, q), device_id_type=MESH,
        )

    def project(h, *places):
        chips = [at(*d) for d in places]
        p = dot(jnp.concatenate([att[h][q] for q in chips], axis=0), ow[...]).astype(BF)
        for n, q in enumerate(chips):
            rows = p[n * PART[h] : (n + 1) * PART[h]]
            proj_s[h][q, 0] = rows[:, :FEAT]
            proj_s[h][q, 1] = rows[:, FEAT:]
            proj_copy(h, q, 1 - core, e).start()

            @pl.when(q != e)
            def _():
                proj_copy(h, q, core, e).start()

    project(0, (0, 0))
    project(1, (0, 0))
    for h in range(2):
        att_come(h, 0, 1)
        att_come(h, 2, 0)
        att_come(h, 1, 0)
        att_come(h, 3, 0)
        project(h, (0, 1), (2, 0), (1, 0), (3, 0))
    for h in range(2):
        att_come(h, 1, 1)
        att_come(h, 3, 1)
        att_come(h, 2, 1)
        project(h, (1, 1), (3, 1), (2, 1))

    l_resid.wait()
    total = []
    for h in range(2):
        proj_r[h][e, core] = proj_s[h][e, core]
        for k in range(EXP):
            src = lax.rem(e + k, EXP)
            for c in (1 - core, core)[: 1 if k == 0 else 2]:
                arrive(proj_r[h].at[src, c], proj_rs.at[h, src, c])
    for c in range(2):
        for h in range(2):
            low = c * SROWS + FIRST[h]
            t = resid[low : low + PART[h], :].astype(F32)
            for src in range(EXP):
                t = t + proj_r[h][src, c].astype(F32)
            total.append(t)
    hid = jnp.concatenate(total, axis=0).astype(BF)
    hidden[...] = hid

    z, yl = e // 2, lax.rem(e, 2)

    def block_at(dz, dy):
        return lax.rem(z + dz, 4) * 2 + lax.rem(yl + dy, 2)

    disp_s[...] = dot(picker[...], hid).astype(BF).reshape(EXP, CAPP, FEAT)
    for i in range(1, EXP):
        dz, dy = NEAR[i]
        p = NEAR.index(((4 - dz) % 4, dy))
        d = block_at(dz, dy)
        cp = pltpu.make_async_remote_copy(
            disp_s.at[d], big.at[p // 4, s, pl.ds(p % 4 * CAPP, CAPP)], disp_ss.at[i], disp_rs.at[p],
            device_id=(s, d), device_id_type=MESH,
        )
        cp.start()
        pending.append(cp)
    big[0, s, :CAPP, :] = disp_s[e]

    def dispatched(h):
        for p in range(max(1, h * 4), h * 4 + 4):
            pltpu.make_async_remote_copy(
                disp_s.at[0], big.at[h, s, pl.ds(p % 4 * CAPP, CAPP)], disp_ss.at[0], disp_rs.at[p],
                device_id=(s, block_at(*NEAR[p])), device_id_type=MESH,
            ).wait_recv()

    count = [0]

    def send(src, sem, dest):
        cp = pltpu.make_async_remote_copy(
            src, src, big_ss.at[count[0]], sem, device_id=dest, device_id_type=MESH
        )
        cp.start()
        count[0] += 1
        pending.append(cp)

    def part(h, slot, k):
        return big.at[h, slot, pl.ds(k * HALF // 2, HALF // 2)]

    def start_half(h):
        for d in ((0, 1), (1, 0), (3, 0)):
            send(big.at[h, s], big_rs.at[h, s], lane(at(*d)))
        send(big.at[h, s], big_rs.at[h, s], other)

    def come(h, dx, dy):
        q = at(dx, dy)
        slot = q * 2 + core
        whole = big.at[h, slot]
        if (dx, dy) == (2, 0):
            arrive(part(h, slot, 0), part_rs.at[h, 0])
            arrive(part(h, slot, 1), part_rs.at[h, 1])
            send(whole, big_rs.at[h, slot], lane(at(0, 1)))
        else:
            arrive(whole, big_rs.at[h, slot])
        if (dx, dy) == (0, 1):
            send(whole, big_rs.at[h, slot], lane(at(1, 0)))
            send(whole, big_rs.at[h, slot], lane(at(3, 0)))
        if (dx, dy) == (3, 0):
            send(part(h, slot, 0), part_rs.at[h, 0], lane(at(1, 0)))
        if (dx, dy) == (1, 0):
            send(part(h, slot, 1), part_rs.at[h, 1], lane(at(3, 0)))
        send(whole, big_rs.at[h, slot], other)

    begun = [False, False]

    def up(h, *d):
        q = at(*d)
        theirs = q * 2 + 1 - core
        arrive(big.at[h, theirs], big_rs.at[h, theirs])
        rows = jnp.concatenate([big[h, q * 2], big[h, q * 2 + 1]], axis=1)
        feats = pl.ds(pl.multiple_of(q * 2 * FEAT, 2 * FEAT), 2 * FEAT)
        ga, ua = dot(rows, wg[feats, :]), dot(rows, wu[feats, :])
        if begun[h]:
            acc[h, 0] += ga
            acc[h, 1] += ua
        else:
            acc[h, 0] = ga
            acc[h, 1] = ua
        begun[h] = True

    def activate(h):
        g = acc[h, 0]
        act[h] = (g / (1.0 + jnp.exp(-g)) * acc[h, 1]).astype(BF)

    def down(h, i):
        p = dot(act[h], wd[at(*ORDER[i])])
        lo, hi = p[:, :FEAT], p[:, FEAT:]
        mine[h, i] = jnp.where(core == 0, lo, hi)
        pair_s[h, i] = jnp.where(core == 0, hi, lo).astype(BF)
        cp = pltpu.make_async_remote_copy(
            pair_s.at[h, i], pair_r.at[h, i], pair_ss.at[h, i], pair_rs.at[h, i], device_id=other, device_id_type=MESH
        )
        cp.start()
        pending.append(cp)

    def landed(buf, rs, h, j):
        pltpu.make_async_remote_copy(
            buf.at[h, j], buf.at[h, j], red_ss.at[0, 0], rs.at[h, j], device_id=other, device_id_type=MESH
        ).wait_recv()
        return buf[h, j].astype(F32)

    def push(h, i, src, dst, sem, dest):
        cp = pltpu.make_async_remote_copy(
            src, dst, red_ss.at[h, i], sem, device_id=lane(at(*dest)), device_id_type=MESH
        )
        cp.start()
        pending.append(cp)

    def finish(h, i):
        v = mine[h, i] + landed(pair_r, pair_rs, h, i)
        if i == 3:
            v = v + landed(mid_r, mid_rs, h, 2)
        if i == 6:
            v = v + landed(mid_r, mid_rs, h, 0) + landed(mid_r, mid_rs, h, 1)
        out = red_s.at[h, i]
        if i == 4:
            red_s[h, i, : HALF // 2] = v[: HALF // 2].astype(BF)
            red_s[h, i, HALF // 2 :] = (v[HALF // 2 :] + landed(hop_r, hop_rs, h, 1)).astype(BF)
        elif i == 5:
            red_s[h, i, : HALF // 2] = (v[: HALF // 2] + landed(hop_r, hop_rs, h, 0)).astype(BF)
            red_s[h, i, HALF // 2 :] = v[HALF // 2 :].astype(BF)
        elif i < 7:
            red_s[h, i] = v.astype(BF)
        if i == 0:
            push(h, i, out, mid_r.at[h, 2], mid_rs.at[h, 2], (0, 1))
        elif i == 1:
            push(h, i, out, mid_r.at[h, 0], mid_rs.at[h, 0], (1, 0))
        elif i == 2:
            push(h, i, out, mid_r.at[h, 1], mid_rs.at[h, 1], (3, 0))
        elif i == 3:
            push(h, i, out.at[pl.ds(0, HALF // 2)], hop_r.at[h, 0], hop_rs.at[h, 0], (3, 0))
            push(h, 7, out.at[pl.ds(HALF // 2, HALF // 2)], hop_r.at[h, 1], hop_rs.at[h, 1], (1, 0))
        elif i == 4:
            push(h, i, out, fin_r.at[h, 0], fin_rs.at[h, 0], (1, 0))
        elif i == 5:
            push(h, i, out, fin_r.at[h, 1], fin_rs.at[h, 1], (3, 0))
        elif i == 6:
            push(h, i, out, fin_r.at[h, 2], fin_rs.at[h, 2], (0, 1))
        else:
            for j in range(3):
                v = v + landed(fin_r, fin_rs, h, j)
            ret_s[h] = v.astype(BF)
            for p in range(max(1, h * 4), h * 4 + 4):
                d = block_at(*NEAR[p])
                cp = pltpu.make_async_remote_copy(
                    ret_s.at[h, pl.ds(p % 4 * CAPP, CAPP)], ret.at[e], ret_ss.at[p], ret_rs.at[e],
                    device_id=(s, d), device_id_type=MESH,
                )
                cp.start()
                pending.append(cp)
            if h == 0:
                ret[e] = ret_s[0, :CAPP]

    dispatched(0)
    start_half(0)
    dispatched(1)
    start_half(1)
    l_wg.wait()
    l_wu.wait()
    up(0, 0, 0)
    up(1, 0, 0)
    for h in range(2):
        come(h, 1, 0)
        come(h, 3, 0)
    for h in range(2):
        come(h, 0, 1)
    up(0, 1, 0)
    up(0, 3, 0)
    up(0, 0, 1)
    come(0, 2, 0)
    up(1, 1, 0)
    up(1, 3, 0)
    come(1, 2, 0)
    up(1, 0, 1)
    up(0, 2, 0)
    come(0, 1, 1)
    come(0, 3, 1)
    up(1, 2, 0)
    come(1, 1, 1)
    come(1, 3, 1)
    up(0, 1, 1)
    up(0, 3, 1)
    come(0, 2, 1)
    up(1, 1, 1)
    up(1, 3, 1)
    up(0, 2, 1)
    activate(0)
    for cp in l_wd:
        cp.wait()
    down(0, 0)
    down(0, 1)
    finish(0, 0)
    down(0, 2)
    finish(0, 1)
    finish(0, 2)
    come(1, 2, 1)
    up(1, 2, 1)
    activate(1)
    down(1, 0)
    down(1, 1)
    finish(1, 0)
    down(1, 2)
    finish(1, 1)
    finish(1, 2)
    down(0, 3)
    finish(0, 3)
    down(1, 3)
    down(0, 6)
    down(0, 4)
    down(0, 5)
    finish(1, 3)
    finish(0, 6)
    down(1, 6)
    down(1, 4)
    down(1, 5)
    finish(0, 4)
    finish(0, 5)
    finish(1, 6)
    down(0, 7)
    down(1, 7)
    finish(1, 4)
    finish(1, 5)
    finish(0, 7)
    finish(1, 7)

    for k in range(1, EXP):
        src = lax.rem(e + k, EXP)
        pltpu.make_async_remote_copy(
            ret.at[src], ret.at[src], ret_ss.at[0], ret_rs.at[src], device_id=(s, src), device_id_type=MESH
        ).wait_recv()
    back = ret[...].reshape(BUF, FEAT)
    out_ref[...] = hidden[...].astype(F32) + (dot(comb[0], back) + dot(comb[1], back))

    for cp in pending:
        cp.wait_send()
    for h in range(2):
        for k in range(EXP):
            d = lax.rem(e + k, EXP)
            for c in (1 - core, core)[: 1 if k == 0 else 2]:
                proj_copy(h, d, c, e).wait_send()


def per_device(
    resid, query, new_keys, new_values, cache_keys, cache_values, cache_len, out_weight,
    expert_ids, gates, w_gate, w_up, w_down,
):
    pick, mask, back0, back1 = constants()
    V = pltpu.VMEM
    S = pltpu.SemaphoreType.DMA
    scratch = [
        V((BLK, FEAT), BF), V((SROWS, 768), BF), V((SROWS, HD), BF), V((SROWS, HD), BF),
        V((REQS, CACHE, HD), BF), V((REQS, CACHE, HD), BF), V((768, 2 * FEAT), BF),
        V((2, EXP * BLK), jnp.int32), V((2, BLK), F32),
        V((D, HID), BF), V((D, HID), BF), V((CHIPS, HID, 2 * FEAT), BF),
        V(pick.shape, BF), V(back0.shape, BF), V(back1.shape, BF), V(mask.shape, F32),
        V((REQS * PADQ, HD), BF), V((REQS * PADQ, SROWS), F32),
        V((REQS * PADQ, HD), BF), V((CHIPS, PART[0], 768), BF), V((CHIPS, PART[1], 768), BF),
        V((EXP, 2, PART[0], FEAT), BF), V((EXP, 2, PART[1], FEAT), BF),
        V((EXP, 2, PART[0], FEAT), BF), V((EXP, 2, PART[1], FEAT), BF),
        V((BLK, FEAT), BF), V((BUF, BLK), BF), V((2, BLK, BUF), BF),
        V((EXP, CAPP, FEAT), BF), V((2, SEC, HALF, FEAT), BF),
        V((2, 2, HALF, HID), F32), V((2, HALF, HID), BF),
        V((2, CHIPS, HALF, FEAT), BF), V((2, CHIPS, HALF, FEAT), BF), V((2, CHIPS, HALF, FEAT), F32),
        V((2, CHIPS, HALF, FEAT), BF), V((2, 3, HALF, FEAT), BF),
        V((2, 2, HALF // 2, FEAT), BF), V((2, 3, HALF, FEAT), BF),
        V((2, HALF, FEAT), BF), V((EXP, CAPP, FEAT), BF),
        S((37,)), S, S, S((2, 7)), S((2, CHIPS)), S((2, EXP, 2)), S((2, EXP, 2)), S((EXP,)), S((EXP,)), S((40,)), S((2, SEC)), S((2, 2)),
        S((2, CHIPS)), S((2, CHIPS)), S((2, CHIPS)), S((2, 3)), S((2, 2)), S((2, 3)), S((EXP,)), S((EXP,)),
    ]
    anyspec = pl.BlockSpec(memory_space=pl.ANY)
    out = pl.pallas_call(
        kernel,
        out_shape=jax.ShapeDtypeStruct((BLK, FEAT), F32),
        in_specs=[pl.BlockSpec(memory_space=pltpu.SMEM)] + [anyspec] * 16,
        out_specs=pl.BlockSpec(memory_space=pltpu.VMEM),
        scratch_shapes=scratch,
        compiler_params=pltpu.CompilerParams(collective_id=0, has_side_effects=True, vmem_limit_bytes=60 << 20),
    )(
        cache_len, resid, query, new_keys, new_values, cache_keys, cache_values, out_weight, expert_ids.T, gates.T,
        w_gate, w_up, w_down, jnp.asarray(pick, BF), jnp.asarray(back0, BF), jnp.asarray(back1, BF), jnp.asarray(mask, F32),
    )
    return out.astype(BF)


def solution(mesh):
    in_specs = (
        P("expert", "section"),
        P("section", "expert"),
        P("section", "expert"),
        P("section", "expert"),
        P("section", None, "expert"),
        P("section", None, "expert"),
        P("section"),
        P("expert", "section"),
        P(),
        P("expert", None),
        P("expert", None, "section"),
        P("expert", None, "section"),
        P("expert", "section", None),
    )
    return jax.shard_map(
        per_device, mesh=mesh, in_specs=in_specs, out_specs=P("expert", "section"), check_vma=False
    )
```

```python
import functools
import math

import jax
import jax.numpy as jnp
import numpy as np
from jax import lax
from jax.experimental import pallas as pl
from jax.experimental.pallas import tpu as pltpu
from jax.sharding import PartitionSpec as P

MESH = pl.DeviceIdType.MESH
BF = jnp.bfloat16
F32 = jnp.float32

GROUPS = 6
HD = 128
DRAFT = 6
REQS = 8
SROWS = 48
PADQ = 48
CACHE = 1024
BLK = 96
CAPP = 32
EXP = 8
CHIPS = 8
SEC = 16
BUF = EXP * CAPP
FEAT = 384
D = 6144
HID = 512
HALF = BUF // 2
QUART = BUF // 4
NEG = -1e30
PART, FIRST, HOLD = (32, 16), (0, 32), ((0, 6), (5, 8))
NEAR = [(0, 0), (0, 1), (1, 0), (3, 0), (1, 1), (3, 1), (2, 0), (2, 1)]
ORDER = [(2, 1), (1, 1), (3, 1), (2, 0), (1, 0), (3, 0), (0, 1), (0, 0)]


def constants():
    pick = np.zeros((REQS * PADQ, GROUPS * SROWS), np.float32)
    mask = np.zeros((REQS * PADQ, SROWS), np.float32)
    for r in range(REQS):
        for g in range(GROUPS):
            for d in range(DRAFT):
                i = r * PADQ + g * DRAFT + d
                pick[i, g * SROWS + r * DRAFT + d] = 1.0
                mask[i, r * DRAFT : r * DRAFT + d + 1] = 1.0
    back = []
    for rows, first, (low, high) in zip(PART, FIRST, HOLD):
        cut = pick[low * PADQ : high * PADQ].reshape(-1, GROUPS, SROWS)[:, :, first : first + rows]
        back.append(cut.reshape(-1, GROUPS * rows).T)
    return pick, mask, *back


def dot(a, b):
    return jnp.dot(a, b, preferred_element_type=F32)


def dot_t(a, b):
    return lax.dot_general(a, b, (((1,), (1,)), ((), ())), preferred_element_type=F32)


def kernel(
    clen,
    resid_h, query_h, nk_h, nv_h, ck_h, cv_h, ow_h, ids_h, gates_h, wg_h, wu_h, wd_h, pick_h, back0_h, back1_h, mask_h,
    out_ref,
    resid, query, nk, nv, ck, cv, ow, ids, gates, wg, wu, wd, pick, back0, back1, mask,
    qp, snew, mixed, att0, att1, proj_s0, proj_s1, proj_r0, proj_r1, hidden, picker, comb, disp_s, big, acc, act,
    pair_s, pair_r, mine, red_s, mid_r, hop_r, fin_r, ret_s, ret,
    lsem, ow_ss, ow_rs, att_ss, att_rs, proj_ss, proj_rs, disp_ss, disp_rs, big_ss, big_rs, part_rs,
    pair_ss, pair_rs, red_ss, mid_rs, hop_rs, fin_rs, ret_ss, ret_rs,
):
    s = lax.axis_index("section")
    e = lax.axis_index("expert")
    core = lax.rem(s, 2)
    chip = s // 2
    x, yh = chip // 2, lax.rem(chip, 2)

    def at(dx, dy):
        return lax.rem(x + dx + 4, 4) * 2 + lax.rem(yh + dy, 2)

    def lane(q):
        return (q * 2 + core, e)

    other = (chip * 2 + 1 - core, e)

    loads = [(query_h, query), (pick_h, pick), (nk_h, nk), (mask_h, mask)]
    loads += [(ck_h.at[r], ck.at[r]) for r in range(REQS)]
    loads += [(nv_h, nv)]
    loads += [(cv_h.at[r], cv.at[r]) for r in range(REQS)]
    mine_ow = ow.at[:, pl.ds(pl.multiple_of(core * FEAT, HD), FEAT)]
    loads += [(back0_h, back0), (back1_h, back1), (ow_h, mine_ow), (ids_h, ids), (gates_h, gates), (resid_h, resid)]
    early = len(loads)
    loads += [(wg_h.at[0], wg), (wu_h.at[0], wu)]
    loads += [(wd_h.at[0, :, pl.ds(q * 2 * FEAT, 2 * FEAT)], wd.at[q]) for q in range(CHIPS)]
    local = [pltpu.make_async_copy(a, b, lsem.at[i]) for i, (a, b) in enumerate(loads)]
    for cp in local[:early]:
        cp.start()
    (l_query, l_pick, l_nk, l_mask), l_ck = local[:4], local[4:12]
    l_nv, l_cv = local[12], local[13:21]
    l_back, l_ow, l_ids, l_gates, l_resid, l_wg, l_wu = local[21:23], *local[23:29]
    l_wd = local[29:37]

    bar = pltpu.get_barrier_semaphore()
    ring = [(1, 0), (3, 0), (2, 0), (0, 1)]
    partners = [lane(at(dx, dy)) for dx, dy in ring] + [other]
    partners += [(d, lax.rem(e + k, EXP)) for k in range(1, EXP) for d in (s, other[0])]
    for p in partners:
        pl.semaphore_signal(bar, 1, device_id=p, device_id_type=MESH)

    l_query.wait()
    l_pick.wait()
    stacked = jnp.concatenate([query[:, g * HD : (g + 1) * HD] for g in range(GROUPS)], axis=0)
    qp[...] = dot(pick[...], stacked).astype(BF)
    l_nk.wait()
    l_mask.wait()
    scale = 1.0 / math.sqrt(HD)
    snew[...] = jnp.where(mask[...] > 0.5, dot_t(qp[...], nk[...]) * scale, NEG)
    col = lax.broadcasted_iota(jnp.int32, (PADQ, CACHE), 1)
    l_nv.wait()

    def attend(r):
        l_ck[r].wait()
        rows = pl.ds(r * PADQ, PADQ)
        sc = dot_t(qp[rows, :], ck[r]) * scale
        sc = jnp.where(col < clen[r], sc, NEG)
        sn = snew[rows, :]
        top = jnp.maximum(jnp.max(sc, axis=1, keepdims=True), jnp.max(sn, axis=1, keepdims=True))
        pe = jnp.exp(sc - top)
        ne = jnp.exp(sn - top)
        inv = 1.0 / (jnp.sum(pe, axis=1, keepdims=True) + jnp.sum(ne, axis=1, keepdims=True))
        l_cv[r].wait()
        mixed[rows, :] = (dot((pe * inv).astype(BF), cv[r]) + dot((ne * inv).astype(BF), nv[...])).astype(BF)

    att = (att0, att1)
    pending = []

    def arrive(dst, sem):
        pltpu.make_async_remote_copy(dst, dst, ow_ss, sem, device_id=other, device_id_type=MESH).wait_recv()

    def att_send(h, q, n, dest):
        piece = att[h].at[q]
        cp = pltpu.make_async_remote_copy(
            piece, piece, att_ss.at[h, n], att_rs.at[h, q], device_id=lane(at(*dest)), device_id_type=MESH
        )
        cp.start()
        pending.append(cp)

    def att_start(h):
        l_back[h].wait()
        low, high = HOLD[h]
        spread = dot((back0, back1)[h][...], mixed[low * PADQ : high * PADQ, :]).astype(BF)
        n = PART[h]
        for g in range(GROUPS):
            att[h][chip, :, g * HD : (g + 1) * HD] = spread[g * n : (g + 1) * n]
        for n, d in enumerate(((0, 1), (2, 0), (1, 0), (3, 0))):
            att_send(h, chip, n, d)

    def att_come(h, *d):
        q = at(*d)
        arrive(att[h].at[q], att_rs.at[h, q])
        if d == (0, 1):
            att_send(h, q, 4, (1, 0))
            att_send(h, q, 5, (3, 0))
        if d == (2, 0):
            att_send(h, q, 6, (0, 1))

    for r in range(HOLD[0][1]):
        attend(r)
    pl.semaphore_wait(bar, len(partners))
    l_ow.wait()
    cp = pltpu.make_async_remote_copy(mine_ow, mine_ow, ow_ss, ow_rs, device_id=other, device_id_type=MESH)
    cp.start()
    pending.append(cp)
    att_start(0)
    for r in range(HOLD[0][1], REQS):
        attend(r)
    att_start(1)
    for cp in local[early:]:
        cp.start()

    proj_s, proj_r = (proj_s0, proj_s1), (proj_r0, proj_r1)
    their_ow = ow.at[:, pl.ds(pl.multiple_of((1 - core) * FEAT, HD), FEAT)]
    arrive(their_ow, ow_rs)

    def proj_copy(h, q, c, frm):
        return pltpu.make_async_remote_copy(
            proj_s[h].at[q, c], proj_r[h].at[frm, core], proj_ss.at[h, q, c], proj_rs.at[h, frm, core],
            device_id=(chip * 2 + c, q), device_id_type=MESH,
        )

    def project(h, *places):
        chips = [at(*d) for d in places]
        p = dot(jnp.concatenate([att[h][q] for q in chips], axis=0), ow[...]).astype(BF)
        for n, q in enumerate(chips):
            rows = p[n * PART[h] : (n + 1) * PART[h]]
            proj_s[h][q, 0] = rows[:, :FEAT]
            proj_s[h][q, 1] = rows[:, FEAT:]
            proj_copy(h, q, 1 - core, e).start()

            @pl.when(q != e)
            def _():
                proj_copy(h, q, core, e).start()

    project(0, (0, 0))
    project(1, (0, 0))
    for h in range(2):
        att_come(h, 0, 1)
        att_come(h, 2, 0)
    for h in range(2):
        att_come(h, 1, 0)
        att_come(h, 3, 0)
        project(h, (0, 1), (2, 0), (1, 0), (3, 0))
    for h in range(2):
        att_come(h, 1, 1)
        att_come(h, 3, 1)
        att_come(h, 2, 1)
        project(h, (1, 1), (3, 1), (2, 1))

    l_ids.wait()
    l_gates.wait()
    of_block = lax.broadcasted_iota(jnp.int32, (EXP * BLK, BLK), 0) == (
        lax.broadcasted_iota(jnp.int32, (EXP * BLK, BLK), 1) + e * BLK
    )
    named_by = dot(ids[...].astype(F32).astype(BF), jnp.where(of_block, 1.0, 0.0).astype(BF))
    jv = lax.broadcasted_iota(jnp.int32, (BUF, BLK), 0)
    expert_of = (jv // CAPP).astype(F32)
    slot_of = lax.rem(jv, CAPP).astype(F32)
    n0 = named_by[0:1, :] == expert_of
    n1 = named_by[1:2, :] == expert_of
    named = jnp.where(n0 | n1, 1.0, 0.0)
    upper = lax.broadcasted_iota(jnp.int32, (BLK, BLK), 0) < lax.broadcasted_iota(jnp.int32, (BLK, BLK), 1)
    earlier = dot(named.astype(BF), jnp.where(upper, 1.0, 0.0).astype(BF))
    place = jnp.where(earlier == slot_of, named, 0.0)
    picker[...] = place.astype(BF)
    weight = jnp.transpose(place * (jnp.where(n0, gates[0:1, :], 0.0) + jnp.where(n1, gates[1:2, :], 0.0)))
    comb[0] = weight.astype(BF)
    comb[1] = (weight - comb[0].astype(F32)).astype(BF)

    l_resid.wait()
    total = []
    for h in range(2):
        proj_r[h][e, core] = proj_s[h][e, core]
        for k in range(EXP):
            src = lax.rem(e + k, EXP)
            for c in (1 - core, core)[: 1 if k == 0 else 2]:
                arrive(proj_r[h].at[src, c], proj_rs.at[h, src, c])
    for c in range(2):
        for h in range(2):
            low = c * SROWS + FIRST[h]
            t = resid[low : low + PART[h], :].astype(F32)
            for src in range(EXP):
                t = t + proj_r[h][src, c].astype(F32)
            total.append(t)
    hid = jnp.concatenate(total, axis=0).astype(BF)
    hidden[...] = hid

    z, yl = e // 2, lax.rem(e, 2)

    def block_at(dz, dy):
        return lax.rem(z + dz, 4) * 2 + lax.rem(yl + dy, 2)

    disp_s[...] = dot(picker[...], hid).astype(BF).reshape(EXP, CAPP, FEAT)
    for i in range(1, EXP):
        dz, dy = NEAR[i]
        p = NEAR.index(((4 - dz) % 4, dy))
        d = block_at(dz, dy)
        cp = pltpu.make_async_remote_copy(
            disp_s.at[d], big.at[p // 4, s, pl.ds(p % 4 * CAPP, CAPP)], disp_ss.at[i], disp_rs.at[p],
            device_id=(s, d), device_id_type=MESH,
        )
        cp.start()
        pending.append(cp)
    big[0, s, :CAPP, :] = disp_s[e]

    def dispatched(n):
        for p in range(max(1, 2 * n), 2 * n + 2):
            arrive(big.at[p // 4, s, pl.ds(p % 4 * CAPP, CAPP)], disp_rs.at[p])

    count = [0]

    def send(src, sem, dest):
        cp = pltpu.make_async_remote_copy(
            src, src, big_ss.at[count[0]], sem, device_id=dest, device_id_type=MESH
        )
        cp.start()
        count[0] += 1
        pending.append(cp)

    def piece(n, slot, k=0, rows=QUART):
        return big.at[n // 2, slot, pl.ds(n % 2 * QUART + k * rows, rows)]

    def start(n):
        dispatched(n)
        for d in ((1, 0), (3, 0), (0, 1)):
            send(piece(n, s), big_rs.at[n, s], lane(at(*d)))
        send(piece(n, s), big_rs.at[n, s], other)

    def come(n, *d):
        q = at(*d)
        slot = q * 2 + core
        whole, parts = piece(n, slot), [piece(n, slot, k, QUART // 2) for k in range(2)]
        sem = big_rs.at[n, slot]
        if d == (2, 0):
            arrive(parts[0], part_rs.at[n, 0])
            arrive(parts[1], part_rs.at[n, 1])
            send(whole, sem, lane(at(0, 1)))
        else:
            arrive(whole, sem)
        if d == (0, 1):
            send(whole, sem, lane(at(1, 0)))
            send(whole, sem, lane(at(3, 0)))
        if d == (3, 0):
            send(parts[0], part_rs.at[n, 0], lane(at(1, 0)))
        if d == (1, 0):
            send(parts[1], part_rs.at[n, 1], lane(at(3, 0)))
        send(whole, sem, other)

    begun = [False, False]

    def up(h, *d):
        q = at(*d)
        theirs = q * 2 + 1 - core
        for n in (2 * h, 2 * h + 1):
            arrive(piece(n, theirs), big_rs.at[n, theirs])
        rows = jnp.concatenate([big[h, q * 2], big[h, q * 2 + 1]], axis=1)
        feats = pl.ds(pl.multiple_of(q * 2 * FEAT, 2 * FEAT), 2 * FEAT)
        ga, ua = dot(rows, wg[feats, :]), dot(rows, wu[feats, :])
        if begun[h]:
            acc[h, 0] += ga
            acc[h, 1] += ua
        else:
            acc[h, 0] = ga
            acc[h, 1] = ua
        begun[h] = True

    def activate(h):
        g = acc[h, 0]
        act[h] = (g / (1.0 + jnp.exp(-g)) * acc[h, 1]).astype(BF)

    def down(h, i):
        p = dot(act[h], wd[at(*ORDER[i])])
        lo, hi = p[:, :FEAT], p[:, FEAT:]
        mine[h, i] = jnp.where(core == 0, lo, hi)
        pair_s[h, i] = jnp.where(core == 0, hi, lo).astype(BF)
        cp = pltpu.make_async_remote_copy(
            pair_s.at[h, i], pair_r.at[h, i], pair_ss.at[h, i], pair_rs.at[h, i], device_id=other, device_id_type=MESH
        )
        cp.start()
        pending.append(cp)

    def landed(buf, rs, h, j):
        pltpu.make_async_remote_copy(
            buf.at[h, j], buf.at[h, j], red_ss.at[0, 0], rs.at[h, j], device_id=other, device_id_type=MESH
        ).wait_recv()
        return buf[h, j].astype(F32)

    def push(h, i, src, dst, sem, dest):
        cp = pltpu.make_async_remote_copy(
            src, dst, red_ss.at[h, i], sem, device_id=lane(at(*dest)), device_id_type=MESH
        )
        cp.start()
        pending.append(cp)

    def finish(h, i):
        v = mine[h, i] + landed(pair_r, pair_rs, h, i)
        if i == 3:
            v = v + landed(mid_r, mid_rs, h, 2)
        if i == 6:
            v = v + landed(mid_r, mid_rs, h, 0) + landed(mid_r, mid_rs, h, 1)
        out = red_s.at[h, i]
        if i == 4:
            red_s[h, i, : HALF // 2] = v[: HALF // 2].astype(BF)
            red_s[h, i, HALF // 2 :] = (v[HALF // 2 :] + landed(hop_r, hop_rs, h, 1)).astype(BF)
        elif i == 5:
            red_s[h, i, : HALF // 2] = (v[: HALF // 2] + landed(hop_r, hop_rs, h, 0)).astype(BF)
            red_s[h, i, HALF // 2 :] = v[HALF // 2 :].astype(BF)
        elif i < 7:
            red_s[h, i] = v.astype(BF)
        if i == 0:
            push(h, i, out, mid_r.at[h, 2], mid_rs.at[h, 2], (0, 1))
        elif i == 1:
            push(h, i, out, mid_r.at[h, 0], mid_rs.at[h, 0], (1, 0))
        elif i == 2:
            push(h, i, out, mid_r.at[h, 1], mid_rs.at[h, 1], (3, 0))
        elif i == 3:
            push(h, i, out.at[pl.ds(0, HALF // 2)], hop_r.at[h, 0], hop_rs.at[h, 0], (3, 0))
            push(h, 7, out.at[pl.ds(HALF // 2, HALF // 2)], hop_r.at[h, 1], hop_rs.at[h, 1], (1, 0))
        elif i == 4:
            push(h, i, out, fin_r.at[h, 0], fin_rs.at[h, 0], (1, 0))
        elif i == 5:
            push(h, i, out, fin_r.at[h, 1], fin_rs.at[h, 1], (3, 0))
        elif i == 6:
            push(h, i, out, fin_r.at[h, 2], fin_rs.at[h, 2], (0, 1))
        else:
            for j in range(3):
                v = v + landed(fin_r, fin_rs, h, j)
            ret_s[h] = v.astype(BF)
            for p in range(max(1, h * 4), h * 4 + 4):
                d = block_at(*NEAR[p])
                cp = pltpu.make_async_remote_copy(
                    ret_s.at[h, pl.ds(p % 4 * CAPP, CAPP)], ret.at[e], ret_ss.at[p], ret_rs.at[e],
                    device_id=(s, d), device_id_type=MESH,
                )
                cp.start()
                pending.append(cp)
            if h == 0:
                ret[e] = ret_s[0, :CAPP]

    first, second = (0, 1), (2, 3)
    for n in range(4):
        start(n)
    l_wg.wait()
    l_wu.wait()
    for n in first:
        come(n, 1, 0)
        come(n, 3, 0)
    for n in first:
        come(n, 0, 1)
    up(0, 0, 0)
    for n in second:
        come(n, 1, 0)
        come(n, 3, 0)
    up(0, 1, 0)
    up(0, 3, 0)
    up(0, 0, 1)
    for n in first:
        come(n, 2, 0)
    for n in second:
        come(n, 0, 1)
    up(1, 0, 0)
    up(0, 2, 0)
    for n in first:
        come(n, 1, 1)
        come(n, 3, 1)
    up(1, 1, 0)
    up(1, 3, 0)
    up(1, 0, 1)
    for n in second:
        come(n, 2, 0)
    up(0, 1, 1)
    up(0, 3, 1)
    for n in first:
        come(n, 2, 1)
    up(1, 2, 0)
    for n in second:
        come(n, 1, 1)
        come(n, 3, 1)
    up(0, 2, 1)
    activate(0)
    for cp in l_wd:
        cp.wait()
    down(0, 0)
    down(0, 1)
    finish(0, 0)
    down(0, 2)
    finish(0, 1)
    finish(0, 2)
    up(1, 1, 1)
    up(1, 3, 1)
    for n in second:
        come(n, 2, 1)
    up(1, 2, 1)
    activate(1)
    down(1, 0)
    down(1, 1)
    finish(1, 0)
    down(1, 2)
    finish(1, 1)
    finish(1, 2)
    down(0, 3)
    finish(0, 3)
    down(1, 3)
    down(0, 6)
    down(0, 4)
    down(0, 5)
    finish(1, 3)
    finish(0, 6)
    down(1, 6)
    down(1, 4)
    down(1, 5)
    finish(0, 4)
    finish(0, 5)
    finish(1, 6)
    down(0, 7)
    down(1, 7)
    finish(1, 4)
    finish(1, 5)
    finish(0, 7)
    finish(1, 7)

    for k in range(1, EXP):
        src = lax.rem(e + k, EXP)
        pltpu.make_async_remote_copy(
            ret.at[src], ret.at[src], ret_ss.at[0], ret_rs.at[src], device_id=(s, src), device_id_type=MESH
        ).wait_recv()
    back = ret[...].reshape(BUF, FEAT)
    out_ref[...] = hidden[...].astype(F32) + (dot(comb[0], back) + dot(comb[1], back))

    for cp in pending:
        cp.wait_send()
    for h in range(2):
        for k in range(EXP):
            d = lax.rem(e + k, EXP)
            for c in (1 - core, core)[: 1 if k == 0 else 2]:
                proj_copy(h, d, c, e).wait_send()


def per_device(
    resid, query, new_keys, new_values, cache_keys, cache_values, cache_len, out_weight,
    expert_ids, gates, w_gate, w_up, w_down,
):
    pick, mask, back0, back1 = constants()
    V = pltpu.VMEM
    S = pltpu.SemaphoreType.DMA
    scratch = [
        V((BLK, FEAT), BF), V((SROWS, 768), BF), V((SROWS, HD), BF), V((SROWS, HD), BF),
        V((REQS, CACHE, HD), BF), V((REQS, CACHE, HD), BF), V((768, 2 * FEAT), BF),
        V((2, EXP * BLK), jnp.int32), V((2, BLK), F32),
        V((D, HID), BF), V((D, HID), BF), V((CHIPS, HID, 2 * FEAT), BF),
        V(pick.shape, BF), V(back0.shape, BF), V(back1.shape, BF), V(mask.shape, F32),
        V((REQS * PADQ, HD), BF), V((REQS * PADQ, SROWS), F32),
        V((REQS * PADQ, HD), BF), V((CHIPS, PART[0], 768), BF), V((CHIPS, PART[1], 768), BF),
        V((EXP, 2, PART[0], FEAT), BF), V((EXP, 2, PART[1], FEAT), BF),
        V((EXP, 2, PART[0], FEAT), BF), V((EXP, 2, PART[1], FEAT), BF),
        V((BLK, FEAT), BF), V((BUF, BLK), BF), V((2, BLK, BUF), BF),
        V((EXP, CAPP, FEAT), BF), V((2, SEC, HALF, FEAT), BF),
        V((2, 2, HALF, HID), F32), V((2, HALF, HID), BF),
        V((2, CHIPS, HALF, FEAT), BF), V((2, CHIPS, HALF, FEAT), BF), V((2, CHIPS, HALF, FEAT), F32),
        V((2, CHIPS, HALF, FEAT), BF), V((2, 3, HALF, FEAT), BF),
        V((2, 2, HALF // 2, FEAT), BF), V((2, 3, HALF, FEAT), BF),
        V((2, HALF, FEAT), BF), V((EXP, CAPP, FEAT), BF),
        S((37,)), S, S, S((2, 7)), S((2, CHIPS)), S((2, EXP, 2)), S((2, EXP, 2)), S((EXP,)), S((EXP,)), S((80,)), S((4, SEC)), S((4, 2)),
        S((2, CHIPS)), S((2, CHIPS)), S((2, CHIPS)), S((2, 3)), S((2, 2)), S((2, 3)), S((EXP,)), S((EXP,)),
    ]
    anyspec = pl.BlockSpec(memory_space=pl.ANY)
    out = pl.pallas_call(
        kernel,
        out_shape=pltpu.VMEM((BLK, FEAT), F32),
        in_specs=[pl.BlockSpec(memory_space=pltpu.SMEM)] + [anyspec] * 16,
        out_specs=pl.BlockSpec(memory_space=pltpu.VMEM),
        scratch_shapes=scratch,
        compiler_params=pltpu.CompilerParams(collective_id=0, has_side_effects=True, vmem_limit_bytes=60 << 20),
    )(
        cache_len, resid, query, new_keys, new_values, cache_keys, cache_values, out_weight, expert_ids.T, gates.T,
        w_gate, w_up, w_down, jnp.asarray(pick, BF), jnp.asarray(back0, BF), jnp.asarray(back1, BF), jnp.asarray(mask, F32),
    )
    return out.astype(BF)


def solution(mesh):
    in_specs = (
        P("expert", "section"),
        P("section", "expert"),
        P("section", "expert"),
        P("section", "expert"),
        P("section", None, "expert"),
        P("section", None, "expert"),
        P("section"),
        P("expert", "section"),
        P(),
        P("expert", None),
        P("expert", None, "section"),
        P("expert", None, "section"),
        P("expert", "section", None),
    )
    return jax.shard_map(
        per_device, mesh=mesh, in_specs=in_specs, out_specs=P("expert", "section"), check_vma=False
    )
```

```python
import functools
import math

import jax
import jax.numpy as jnp
import numpy as np
from jax import lax
from jax.experimental import pallas as pl
from jax.experimental.pallas import tpu as pltpu
from jax.sharding import PartitionSpec as P

MESH = pl.DeviceIdType.MESH
BF = jnp.bfloat16
F32 = jnp.float32

GROUPS = 6
HD = 128
DRAFT = 6
REQS = 8
SROWS = 48
PADQ = 48
CACHE = 1024
BLK = 96
CAPP = 32
EXP = 8
CHIPS = 8
SEC = 16
BUF = EXP * CAPP
FEAT = 384
D = 6144
HID = 512
HALF = BUF // 2
QUART = BUF // 4
NEG = -1e30
PART, FIRST, HOLD = (32, 16), (0, 32), ((0, 6), (5, 8))
NEAR = [(0, 0), (0, 1), (1, 0), (3, 0), (1, 1), (3, 1), (2, 0), (2, 1)]
ORDER = [(2, 1), (1, 1), (3, 1), (2, 0), (1, 0), (3, 0), (0, 1), (0, 0)]


def constants():
    pick = np.zeros((REQS * PADQ, GROUPS * SROWS), np.float32)
    mask = np.zeros((REQS * PADQ, SROWS), np.float32)
    for r in range(REQS):
        for g in range(GROUPS):
            for d in range(DRAFT):
                i = r * PADQ + g * DRAFT + d
                pick[i, g * SROWS + r * DRAFT + d] = 1.0
                mask[i, r * DRAFT : r * DRAFT + d + 1] = 1.0
    back = []
    for rows, first, (low, high) in zip(PART, FIRST, HOLD):
        cut = pick[low * PADQ : high * PADQ].reshape(-1, GROUPS, SROWS)[:, :, first : first + rows]
        back.append(cut.reshape(-1, GROUPS * rows).T)
    return pick, mask, *back


def dot(a, b):
    return jnp.dot(a, b, preferred_element_type=F32)


def dot_t(a, b):
    return lax.dot_general(a, b, (((1,), (1,)), ((), ())), preferred_element_type=F32)


def kernel(
    clen,
    resid_h, query_h, nk_h, nv_h, ck_h, cv_h, ow_h, ids_h, gates_h, wg_h, wu_h, wd_h, pick_h, back0_h, back1_h, mask_h,
    out_ref,
    resid, query, nk, nv, ck, cv, ow, ids, gates, wg, wu, wd, pick, back0, back1, mask,
    qp, snew, mixed, att0, att1, proj_s0, proj_s1, proj_r0, proj_r1, hidden, picker, comb, disp_s, big, acc, act,
    pair_s, pair_r, mine, red_s, mid_r, hop_r, fin_r, ret_s, ret,
    lsem, ow_ss, ow_rs, att_ss, att_rs, proj_ss, proj_rs, disp_ss, disp_rs, big_ss, big_rs, part_rs,
    pair_ss, pair_rs, red_ss, mid_rs, hop_rs, fin_rs, ret_ss, ret_rs,
):
    s = lax.axis_index("section")
    e = lax.axis_index("expert")
    core = lax.rem(s, 2)
    chip = s // 2
    x, yh = chip // 2, lax.rem(chip, 2)

    def at(dx, dy):
        return lax.rem(x + dx + 4, 4) * 2 + lax.rem(yh + dy, 2)

    def lane(q):
        return (q * 2 + core, e)

    other = (chip * 2 + 1 - core, e)

    loads = [(query_h, query), (pick_h, pick), (nk_h, nk), (mask_h, mask)]
    loads += [(ck_h.at[r], ck.at[r]) for r in range(REQS)]
    loads += [(nv_h, nv)]
    loads += [(cv_h.at[r], cv.at[r]) for r in range(REQS)]
    mine_ow = ow.at[:, pl.ds(pl.multiple_of(core * FEAT, HD), FEAT)]
    loads += [(back0_h, back0), (back1_h, back1), (ow_h, mine_ow), (ids_h, ids), (gates_h, gates), (resid_h, resid)]
    early = len(loads)
    loads += [(wg_h.at[0], wg), (wu_h.at[0], wu)]
    loads += [(wd_h.at[0, :, pl.ds(q * 2 * FEAT, 2 * FEAT)], wd.at[q]) for q in range(CHIPS)]
    local = [pltpu.make_async_copy(a, b, lsem.at[i]) for i, (a, b) in enumerate(loads)]
    for cp in local[:early]:
        cp.start()
    (l_query, l_pick, l_nk, l_mask), l_ck = local[:4], local[4:12]
    l_nv, l_cv = local[12], local[13:21]
    l_back, l_ow, l_ids, l_gates, l_resid, l_wg, l_wu = local[21:23], *local[23:29]
    l_wd = local[29:37]

    bar = pltpu.get_barrier_semaphore()
    ring = [(1, 0), (3, 0), (2, 0), (0, 1)]
    partners = [lane(at(dx, dy)) for dx, dy in ring] + [other]
    partners += [(d, lax.rem(e + k, EXP)) for k in range(1, EXP) for d in (s, other[0])]
    for p in partners:
        pl.semaphore_signal(bar, 1, device_id=p, device_id_type=MESH)

    l_query.wait()
    l_pick.wait()
    stacked = jnp.concatenate([query[:, g * HD : (g + 1) * HD] for g in range(GROUPS)], axis=0)
    qp[...] = dot(pick[...], stacked).astype(BF)
    l_nk.wait()
    l_mask.wait()
    scale = 1.0 / math.sqrt(HD)
    snew[...] = jnp.where(mask[...] > 0.5, dot_t(qp[...], nk[...]) * scale, NEG)
    col = lax.broadcasted_iota(jnp.int32, (PADQ, CACHE), 1)
    l_nv.wait()

    def attend(r):
        l_ck[r].wait()
        rows = pl.ds(r * PADQ, PADQ)
        sc = dot_t(qp[rows, :], ck[r]) * scale
        sc = jnp.where(col < clen[r], sc, NEG)
        sn = snew[rows, :]
        top = jnp.maximum(jnp.max(sc, axis=1, keepdims=True), jnp.max(sn, axis=1, keepdims=True))
        pe = jnp.exp(sc - top)
        ne = jnp.exp(sn - top)
        inv = 1.0 / (jnp.sum(pe, axis=1, keepdims=True) + jnp.sum(ne, axis=1, keepdims=True))
        l_cv[r].wait()
        mixed[rows, :] = (dot((pe * inv).astype(BF), cv[r]) + dot((ne * inv).astype(BF), nv[...])).astype(BF)

    att = (att0, att1)
    pending = []

    def arrive(dst, sem):
        pltpu.make_async_remote_copy(dst, dst, ow_ss, sem, device_id=other, device_id_type=MESH).wait_recv()

    def att_send(h, q, n, dest):
        piece = att[h].at[q]
        cp = pltpu.make_async_remote_copy(
            piece, piece, att_ss.at[h, n], att_rs.at[h, q], device_id=lane(at(*dest)), device_id_type=MESH
        )
        cp.start()
        pending.append(cp)

    def att_start(h):
        l_back[h].wait()
        low, high = HOLD[h]
        spread = dot((back0, back1)[h][...], mixed[low * PADQ : high * PADQ, :]).astype(BF)
        n = PART[h]
        for g in range(GROUPS):
            att[h][chip, :, g * HD : (g + 1) * HD] = spread[g * n : (g + 1) * n]
        for n, d in enumerate(((0, 1), (2, 0), (1, 0), (3, 0))):
            att_send(h, chip, n, d)

    def att_come(h, *d):
        q = at(*d)
        arrive(att[h].at[q], att_rs.at[h, q])
        if d == (0, 1):
            att_send(h, q, 4, (1, 0))
            att_send(h, q, 5, (3, 0))
        if d == (2, 0):
            att_send(h, q, 6, (0, 1))

    for r in range(HOLD[0][1]):
        attend(r)
    pl.semaphore_wait(bar, len(partners))
    l_ow.wait()
    cp = pltpu.make_async_remote_copy(mine_ow, mine_ow, ow_ss, ow_rs, device_id=other, device_id_type=MESH)
    cp.start()
    pending.append(cp)
    att_start(0)
    for r in range(HOLD[0][1], REQS):
        attend(r)
    att_start(1)
    for cp in local[early:]:
        cp.start()

    proj_s, proj_r = (proj_s0, proj_s1), (proj_r0, proj_r1)
    their_ow = ow.at[:, pl.ds(pl.multiple_of((1 - core) * FEAT, HD), FEAT)]
    arrive(their_ow, ow_rs)

    def proj_copy(h, q, c, frm):
        return pltpu.make_async_remote_copy(
            proj_s[h].at[q, c], proj_r[h].at[frm, core], proj_ss.at[h, q, c], proj_rs.at[h, frm, core],
            device_id=(chip * 2 + c, q), device_id_type=MESH,
        )

    def project(h, *places):
        chips = [at(*d) for d in places]
        p = dot(jnp.concatenate([att[h][q] for q in chips], axis=0), ow[...]).astype(BF)
        for n, q in enumerate(chips):
            rows = p[n * PART[h] : (n + 1) * PART[h]]
            proj_s[h][q, 0] = rows[:, :FEAT]
            proj_s[h][q, 1] = rows[:, FEAT:]
            proj_copy(h, q, 1 - core, e).start()

            @pl.when(q != e)
            def _():
                proj_copy(h, q, core, e).start()

    project(0, (0, 0))
    project(1, (0, 0))
    for h in range(2):
        att_come(h, 0, 1)
        att_come(h, 2, 0)
    for h in range(2):
        att_come(h, 1, 0)
        att_come(h, 3, 0)
        project(h, (0, 1), (2, 0), (1, 0), (3, 0))
    for h in range(2):
        att_come(h, 1, 1)
        att_come(h, 3, 1)
        att_come(h, 2, 1)
        project(h, (1, 1), (3, 1), (2, 1))

    l_ids.wait()
    l_gates.wait()
    of_block = lax.broadcasted_iota(jnp.int32, (EXP * BLK, BLK), 0) == (
        lax.broadcasted_iota(jnp.int32, (EXP * BLK, BLK), 1) + e * BLK
    )
    named_by = dot(ids[...].astype(F32).astype(BF), jnp.where(of_block, 1.0, 0.0).astype(BF))
    jv = lax.broadcasted_iota(jnp.int32, (BUF, BLK), 0)
    expert_of = (jv // CAPP).astype(F32)
    slot_of = lax.rem(jv, CAPP).astype(F32)
    n0 = named_by[0:1, :] == expert_of
    n1 = named_by[1:2, :] == expert_of
    named = jnp.where(n0 | n1, 1.0, 0.0)
    upper = lax.broadcasted_iota(jnp.int32, (BLK, BLK), 0) < lax.broadcasted_iota(jnp.int32, (BLK, BLK), 1)
    earlier = dot(named.astype(BF), jnp.where(upper, 1.0, 0.0).astype(BF))
    place = jnp.where(earlier == slot_of, named, 0.0)
    picker[...] = place.astype(BF)
    weight = jnp.transpose(place * (jnp.where(n0, gates[0:1, :], 0.0) + jnp.where(n1, gates[1:2, :], 0.0)))
    comb[0] = weight.astype(BF)
    comb[1] = (weight - comb[0].astype(F32)).astype(BF)

    l_resid.wait()
    hid = [[None, None], [None, None]]
    for h in range(2):
        proj_r[h][e, core] = proj_s[h][e, core]
        for k in range(EXP):
            src = lax.rem(e + k, EXP)
            for c in (1 - core, core)[: 1 if k == 0 else 2]:
                arrive(proj_r[h].at[src, c], proj_rs.at[h, src, c])
        for c in range(2):
            low = c * SROWS + FIRST[h]
            t = resid[low : low + PART[h], :].astype(F32)
            for src in range(EXP):
                t = t + proj_r[h][src, c].astype(F32)
            hid[c][h] = t
    hid = jnp.concatenate(hid[0] + hid[1], axis=0).astype(BF)
    hidden[...] = hid

    z, yl = e // 2, lax.rem(e, 2)

    def block_at(dz, dy):
        return lax.rem(z + dz, 4) * 2 + lax.rem(yl + dy, 2)

    disp_s[...] = dot(picker[...], hid).astype(BF).reshape(EXP, CAPP, FEAT)
    for i in range(1, EXP):
        dz, dy = NEAR[i]
        p = NEAR.index(((4 - dz) % 4, dy))
        d = block_at(dz, dy)
        cp = pltpu.make_async_remote_copy(
            disp_s.at[d], big.at[p // 4, s, pl.ds(p % 4 * CAPP, CAPP)], disp_ss.at[i], disp_rs.at[p],
            device_id=(s, d), device_id_type=MESH,
        )
        cp.start()
        pending.append(cp)
    big[0, s, :CAPP, :] = disp_s[e]

    def dispatched(n):
        for p in range(max(1, 2 * n), 2 * n + 2):
            arrive(big.at[p // 4, s, pl.ds(p % 4 * CAPP, CAPP)], disp_rs.at[p])

    count = [0]

    def send(src, sem, dest):
        cp = pltpu.make_async_remote_copy(
            src, src, big_ss.at[count[0]], sem, device_id=dest, device_id_type=MESH
        )
        cp.start()
        count[0] += 1
        pending.append(cp)

    def piece(n, slot, k=0, rows=QUART):
        return big.at[n // 2, slot, pl.ds(n % 2 * QUART + k * rows, rows)]

    def start(n):
        dispatched(n)
        for d in ((1, 0), (3, 0), (0, 1)):
            send(piece(n, s), big_rs.at[n, s], lane(at(*d)))
        send(piece(n, s), big_rs.at[n, s], other)

    def come(n, *d):
        q = at(*d)
        slot = q * 2 + core
        whole, parts = piece(n, slot), [piece(n, slot, k, QUART // 2) for k in range(2)]
        sem = big_rs.at[n, slot]
        if d == (2, 0):
            arrive(parts[0], part_rs.at[n, 0])
            arrive(parts[1], part_rs.at[n, 1])
            send(whole, sem, lane(at(0, 1)))
        else:
            arrive(whole, sem)
        if d == (0, 1):
            send(whole, sem, lane(at(1, 0)))
            send(whole, sem, lane(at(3, 0)))
        if d == (3, 0):
            send(parts[0], part_rs.at[n, 0], lane(at(1, 0)))
        if d == (1, 0):
            send(parts[1], part_rs.at[n, 1], lane(at(3, 0)))
        send(whole, sem, other)

    begun = [False, False]

    def up(h, *d):
        q = at(*d)
        theirs = q * 2 + 1 - core
        for n in (2 * h, 2 * h + 1):
            arrive(piece(n, theirs), big_rs.at[n, theirs])
        rows = jnp.concatenate([big[h, q * 2], big[h, q * 2 + 1]], axis=1)
        feats = pl.ds(pl.multiple_of(q * 2 * FEAT, 2 * FEAT), 2 * FEAT)
        ga, ua = dot(rows, wg[feats, :]), dot(rows, wu[feats, :])
        if begun[h]:
            acc[h, 0] += ga
            acc[h, 1] += ua
        else:
            acc[h, 0] = ga
            acc[h, 1] = ua
        begun[h] = True

    def activate(h):
        g = acc[h, 0]
        act[h] = (g / (1.0 + jnp.exp(-g)) * acc[h, 1]).astype(BF)

    def down(h, i):
        p = dot(act[h], wd[at(*ORDER[i])])
        lo, hi = p[:, :FEAT], p[:, FEAT:]
        mine[h, i] = jnp.where(core == 0, lo, hi)
        pair_s[h, i] = jnp.where(core == 0, hi, lo).astype(BF)
        cp = pltpu.make_async_remote_copy(
            pair_s.at[h, i], pair_r.at[h, i], pair_ss.at[h, i], pair_rs.at[h, i], device_id=other, device_id_type=MESH
        )
        cp.start()
        pending.append(cp)

    def landed(buf, rs, h, j):
        pltpu.make_async_remote_copy(
            buf.at[h, j], buf.at[h, j], red_ss.at[0, 0], rs.at[h, j], device_id=other, device_id_type=MESH
        ).wait_recv()
        return buf[h, j].astype(F32)

    def push(h, i, src, dst, sem, dest):
        cp = pltpu.make_async_remote_copy(
            src, dst, red_ss.at[h, i], sem, device_id=lane(at(*dest)), device_id_type=MESH
        )
        cp.start()
        pending.append(cp)

    def finish(h, i):
        v = mine[h, i] + landed(pair_r, pair_rs, h, i)
        if i == 3:
            v = v + landed(mid_r, mid_rs, h, 2)
        if i == 6:
            v = v + landed(mid_r, mid_rs, h, 0) + landed(mid_r, mid_rs, h, 1)
        out = red_s.at[h, i]
        if i == 4:
            red_s[h, i, : HALF // 2] = v[: HALF // 2].astype(BF)
            red_s[h, i, HALF // 2 :] = (v[HALF // 2 :] + landed(hop_r, hop_rs, h, 1)).astype(BF)
        elif i == 5:
            red_s[h, i, : HALF // 2] = (v[: HALF // 2] + landed(hop_r, hop_rs, h, 0)).astype(BF)
            red_s[h, i, HALF // 2 :] = v[HALF // 2 :].astype(BF)
        elif i < 7:
            red_s[h, i] = v.astype(BF)
        if i == 0:
            push(h, i, out, mid_r.at[h, 2], mid_rs.at[h, 2], (0, 1))
        elif i == 1:
            push(h, i, out, mid_r.at[h, 0], mid_rs.at[h, 0], (1, 0))
        elif i == 2:
            push(h, i, out, mid_r.at[h, 1], mid_rs.at[h, 1], (3, 0))
        elif i == 3:
            push(h, i, out.at[pl.ds(0, HALF // 2)], hop_r.at[h, 0], hop_rs.at[h, 0], (3, 0))
            push(h, 7, out.at[pl.ds(HALF // 2, HALF // 2)], hop_r.at[h, 1], hop_rs.at[h, 1], (1, 0))
        elif i == 4:
            push(h, i, out, fin_r.at[h, 0], fin_rs.at[h, 0], (1, 0))
        elif i == 5:
            push(h, i, out, fin_r.at[h, 1], fin_rs.at[h, 1], (3, 0))
        elif i == 6:
            push(h, i, out, fin_r.at[h, 2], fin_rs.at[h, 2], (0, 1))
        else:
            for j in range(3):
                v = v + landed(fin_r, fin_rs, h, j)
            ret_s[h] = v.astype(BF)
            for p in range(max(1, h * 4), h * 4 + 4):
                d = block_at(*NEAR[p])
                cp = pltpu.make_async_remote_copy(
                    ret_s.at[h, pl.ds(p % 4 * CAPP, CAPP)], ret.at[e], ret_ss.at[p], ret_rs.at[e],
                    device_id=(s, d), device_id_type=MESH,
                )
                cp.start()
                pending.append(cp)
            if h == 0:
                ret[e] = ret_s[0, :CAPP]

    first, second = (0, 1), (2, 3)
    for n in range(4):
        start(n)
    l_wg.wait()
    l_wu.wait()
    for n in first:
        come(n, 1, 0)
        come(n, 3, 0)
    for n in first:
        come(n, 0, 1)
    up(0, 0, 0)
    for n in second:
        come(n, 1, 0)
        come(n, 3, 0)
    up(0, 1, 0)
    up(0, 3, 0)
    up(0, 0, 1)
    for n in first:
        come(n, 2, 0)
    for n in second:
        come(n, 0, 1)
    up(1, 0, 0)
    up(0, 2, 0)
    for n in first:
        come(n, 1, 1)
        come(n, 3, 1)
    up(1, 1, 0)
    up(1, 3, 0)
    up(1, 0, 1)
    for n in second:
        come(n, 2, 0)
    up(0, 1, 1)
    up(0, 3, 1)
    for n in first:
        come(n, 2, 1)
    up(1, 2, 0)
    for n in second:
        come(n, 1, 1)
        come(n, 3, 1)
    up(0, 2, 1)
    activate(0)
    for cp in l_wd:
        cp.wait()
    down(0, 0)
    down(0, 1)
    finish(0, 0)
    down(0, 2)
    finish(0, 1)
    finish(0, 2)
    up(1, 1, 1)
    up(1, 3, 1)
    for n in second:
        come(n, 2, 1)
    up(1, 2, 1)
    activate(1)
    down(1, 0)
    down(1, 1)
    finish(1, 0)
    down(1, 2)
    finish(1, 1)
    finish(1, 2)
    down(0, 3)
    finish(0, 3)
    down(1, 3)
    down(0, 6)
    down(0, 4)
    down(0, 5)
    finish(1, 3)
    finish(0, 6)
    down(1, 6)
    down(1, 4)
    down(1, 5)
    finish(0, 4)
    finish(0, 5)
    finish(1, 6)
    down(0, 7)
    down(1, 7)
    finish(1, 4)
    finish(1, 5)
    finish(0, 7)
    finish(1, 7)

    for k in range(1, EXP):
        src = lax.rem(e + k, EXP)
        pltpu.make_async_remote_copy(
            ret.at[src], ret.at[src], ret_ss.at[0], ret_rs.at[src], device_id=(s, src), device_id_type=MESH
        ).wait_recv()
    back = ret[...].reshape(BUF, FEAT)
    out_ref[...] = hidden[...].astype(F32) + (dot(comb[0], back) + dot(comb[1], back))

    for cp in pending:
        cp.wait_send()
    for h in range(2):
        for k in range(EXP):
            d = lax.rem(e + k, EXP)
            for c in (1 - core, core)[: 1 if k == 0 else 2]:
                proj_copy(h, d, c, e).wait_send()


def per_device(
    resid, query, new_keys, new_values, cache_keys, cache_values, cache_len, out_weight,
    expert_ids, gates, w_gate, w_up, w_down,
):
    pick, mask, back0, back1 = constants()
    V = pltpu.VMEM
    S = pltpu.SemaphoreType.DMA
    scratch = [
        V((BLK, FEAT), BF), V((SROWS, 768), BF), V((SROWS, HD), BF), V((SROWS, HD), BF),
        V((REQS, CACHE, HD), BF), V((REQS, CACHE, HD), BF), V((768, 2 * FEAT), BF),
        V((2, EXP * BLK), jnp.int32), V((2, BLK), F32),
        V((D, HID), BF), V((D, HID), BF), V((CHIPS, HID, 2 * FEAT), BF),
        V(pick.shape, BF), V(back0.shape, BF), V(back1.shape, BF), V(mask.shape, F32),
        V((REQS * PADQ, HD), BF), V((REQS * PADQ, SROWS), F32),
        V((REQS * PADQ, HD), BF), V((CHIPS, PART[0], 768), BF), V((CHIPS, PART[1], 768), BF),
        V((EXP, 2, PART[0], FEAT), BF), V((EXP, 2, PART[1], FEAT), BF),
        V((EXP, 2, PART[0], FEAT), BF), V((EXP, 2, PART[1], FEAT), BF),
        V((BLK, FEAT), BF), V((BUF, BLK), BF), V((2, BLK, BUF), BF),
        V((EXP, CAPP, FEAT), BF), V((2, SEC, HALF, FEAT), BF),
        V((2, 2, HALF, HID), F32), V((2, HALF, HID), BF),
        V((2, CHIPS, HALF, FEAT), BF), V((2, CHIPS, HALF, FEAT), BF), V((2, CHIPS, HALF, FEAT), F32),
        V((2, CHIPS, HALF, FEAT), BF), V((2, 3, HALF, FEAT), BF),
        V((2, 2, HALF // 2, FEAT), BF), V((2, 3, HALF, FEAT), BF),
        V((2, HALF, FEAT), BF), V((EXP, CAPP, FEAT), BF),
        S((37,)), S, S, S((2, 7)), S((2, CHIPS)), S((2, EXP, 2)), S((2, EXP, 2)), S((EXP,)), S((EXP,)), S((80,)), S((4, SEC)), S((4, 2)),
        S((2, CHIPS)), S((2, CHIPS)), S((2, CHIPS)), S((2, 3)), S((2, 2)), S((2, 3)), S((EXP,)), S((EXP,)),
    ]
    anyspec = pl.BlockSpec(memory_space=pl.ANY)
    out = pl.pallas_call(
        kernel,
        out_shape=pltpu.VMEM((BLK, FEAT), F32),
        in_specs=[pl.BlockSpec(memory_space=pltpu.SMEM)] + [anyspec] * 16,
        out_specs=pl.BlockSpec(memory_space=pltpu.VMEM),
        scratch_shapes=scratch,
        compiler_params=pltpu.CompilerParams(collective_id=0, has_side_effects=True, vmem_limit_bytes=60 << 20),
    )(
        cache_len, resid, query, new_keys, new_values, cache_keys, cache_values, out_weight, expert_ids.T, gates.T,
        w_gate, w_up, w_down, jnp.asarray(pick, BF), jnp.asarray(back0, BF), jnp.asarray(back1, BF), jnp.asarray(mask, F32),
    )
    return out.astype(BF)


def solution(mesh):
    in_specs = (
        P("expert", "section"),
        P("section", "expert"),
        P("section", "expert"),
        P("section", "expert"),
        P("section", None, "expert"),
        P("section", None, "expert"),
        P("section"),
        P("expert", "section"),
        P(),
        P("expert", None),
        P("expert", None, "section"),
        P("expert", None, "section"),
        P("expert", "section", None),
    )
    return jax.shard_map(
        per_device, mesh=mesh, in_specs=in_specs, out_specs=P("expert", "section"), check_vma=False
    )
```
